256 devices in a mesh: dp: 64 (over z, y_hi, x), tensor: 4 (over y_lo, core).
Axes of the slice: x: 4, y: 4 (y_hi: 2, y_lo: 2; y = y_hi * 2 + y_lo), z: 8, core: 2. Of those that a mesh axis runs over, the one named last changes fastest.
Arguments:
- tokens: bfloat16 [16384, 8192], P('dp'), may hold values from -16 to 16
- gate_weight: bfloat16 [8192, 512], P('dp', 'tensor'), may hold values from -0.0625 to 0.0625
- up_weight: bfloat16 [8192, 512], P('dp', 'tensor'), may hold values from -0.0625 to 0.0625
- down_weight: bfloat16 [512, 8192], P('tensor', 'dp'), may hold values from -0.25 to 0.25
- cotangent: bfloat16 [16384, 8192], P('dp', 'tensor'), may hold values from -16 to 16
Outputs:
- layer_out: bfloat16 [16384, 8192], P('dp', 'tensor')
- token_grad: bfloat16 [16384, 8192], P('dp', 'tensor')
- gate_grad: float32 [8192, 512], P('dp', 'tensor')
- up_grad: float32 [8192, 512], P('dp', 'tensor')
- down_grad: float32 [512, 8192], P('tensor', 'dp')
The draws below stay inside these ranges and needn't reach their ends.
All inputs are finite; a program needn't handle non-finite values.
Results may differ from the reference program's by a relative error of at most 0.013.
Values may be sent and summed in bfloat16 or wider, within the bound.
No kernel may reach another device: no remote copies, remote signals or barrier semaphores. Data moves between devices by JAX's collectives and lax.ppermute only.
A program may use at most 128 MiB of HBM per device.

```python
import jax
import jax.numpy as jnp
from jax import lax

D = 8192
HID = 512
TOKENS = 16384
N_TENSOR = 4


def with_spikes(drawn, key, source, target, shards_of, factor):
    def block_of(axis_at):
        return (jnp.arange(drawn.shape[axis_at]) // (drawn.shape[axis_at] // shards_of)).reshape((-1,) + (1,) * (drawn.ndim - 1 - axis_at))

    near = jax.random.permutation(key, shards_of)[block_of(target)]
    other_side = (block_of(target) + shards_of // 2) % shards_of
    return jnp.where((block_of(source) == near) | (block_of(source) == other_side), factor * drawn, drawn)


def block_levels(own_key, shape, pieces, smallest, top_value):
    factor_of = 1.0
    for axis_at, shards_of in pieces:
        draws = jax.random.uniform(jax.random.fold_in(jax.random.fold_in(own_key, 6), axis_at), (shards_of,), jnp.float32, smallest / len(pieces), top_value / len(pieces))
        factor_of = factor_of * jnp.repeat(jnp.exp(draws), shape[axis_at] // shards_of).reshape((-1,) + (1,) * (len(shape) - 1 - axis_at))
    return factor_of


def noise(key, extent, width, reach, cuts=(), dtype=jnp.bfloat16):
    result = jax.random.normal(key, extent, jnp.float32) * width
    if len(cuts) > 0:
        result = block_levels(key, extent, cuts, -0.22, 0.18) * result
    return jnp.clip(result, min=-reach, max=reach).astype(dtype)


def bell_draw_with(stream_key, shape, deviation, bound, cuts, heavy, kind=jnp.bfloat16):
    drawn = deviation * jax.random.normal(stream_key, shape, jnp.float32)
    if cuts:
        drawn = drawn * block_levels(stream_key, shape, cuts, -0.22, 0.18)
    return jnp.clip(with_spikes(drawn, jax.random.fold_in(stream_key, 3), *heavy), -bound, bound).astype(kind)


def setup_inputs(seed: int = 0) -> dict:
    splits = jax.random.split(jax.random.key(seed), 6)
    return {
        "tokens": bell_draw_with(splits[0], (TOKENS, D), 1.0, 16.0, ((0, 64),), (0, 1, 64, 4.0)),
        "gate_weight": noise(splits[1], (D, HID), D ** -0.5, 0.0625, ((0, 64), (1, 4))),
        "up_weight": noise(splits[2], (D, HID), D ** -0.5, 0.0625, ((0, 64), (1, 4))),
        "down_weight": noise(splits[3], (HID, D), HID ** -0.5, 0.25, ((0, 4), (1, 64))),
        "cotangent": bell_draw_with(splits[4], (TOKENS, D), 1.0, 16.0, ((0, 64), (1, 4)), (0, 1, 64, 4.0)),
    }


def reference(tokens, gate_weight, up_weight, down_weight, cotangent):
    gate_pre = jnp.dot(tokens, gate_weight, preferred_element_type=jnp.float32)
    up_pre = jnp.dot(tokens, up_weight, preferred_element_type=jnp.float32)
    sig_val = jax.nn.sigmoid(gate_pre)
    act_val = gate_pre * sig_val
    hidden = (act_val * up_pre).astype(jnp.bfloat16)
    d_hidden = jnp.dot(cotangent, down_weight.T, preferred_element_type=jnp.float32)
    d_gate = (d_hidden * up_pre * sig_val * (1.0 + gate_pre * (1.0 - sig_val))).astype(jnp.bfloat16)
    d_up = (d_hidden * act_val).astype(jnp.bfloat16)
    group = HID // N_TENSOR
    layer_out = jnp.zeros((TOKENS, D), jnp.float32)
    token_grad = jnp.zeros((TOKENS, D), jnp.float32)
    for index in range(N_TENSOR):
        lower = index * group
        upper = lower + group
        part_out = jnp.dot(hidden[:, lower:upper], down_weight[lower:upper, :], preferred_element_type=jnp.float32).astype(jnp.bfloat16)
        layer_out = layer_out + lax.optimization_barrier(part_out).astype(jnp.float32)
        part_grad = jnp.dot(d_gate[:, lower:upper], gate_weight[:, lower:upper].T, preferred_element_type=jnp.float32)
        part_grad = part_grad + jnp.dot(d_up[:, lower:upper], up_weight[:, lower:upper].T, preferred_element_type=jnp.float32)
        part_grad = part_grad.astype(jnp.bfloat16)
        token_grad = token_grad + lax.optimization_barrier(part_grad).astype(jnp.float32)
    down_grad = jnp.dot(hidden.T, cotangent, preferred_element_type=jnp.float32)
    gate_grad = jnp.dot(tokens.T, d_gate, preferred_element_type=jnp.float32)
    up_grad = jnp.dot(tokens.T, d_up, preferred_element_type=jnp.float32)
    return layer_out.astype(jnp.bfloat16), token_grad.astype(jnp.bfloat16), gate_grad, up_grad, down_grad
```

```python
import jax
import jax.numpy as jnp
from jax import lax
from jax.sharding import PartitionSpec as P

NZ, NH, NX, NL, NC = 8, 2, 4, 2, 2
AXES = ("dp", "tensor")
BF = jnp.bfloat16
F32 = jnp.float32


def index_of(z, h, x, l, c):
    return (((z * NH + h) * NX + x) * NL + l) * NC + c


def pairs_of(move):
    pairs = []
    for z in range(NZ):
        for h in range(NH):
            for x in range(NX):
                for l in range(NL):
                    for c in range(NC):
                        pairs.append((index_of(z, h, x, l, c), index_of(*move(z, h, x, l, c))))
    return pairs


def send(value, move):
    return lax.ppermute(value, AXES, pairs_of(move))


def send_back(value, move):
    return lax.ppermute(value, AXES, [(b, a) for a, b in pairs_of(move)])


def swap_hi(z, h, x, l, c):
    return z, 1 - h, x, l, c


def swap_core(z, h, x, l, c):
    return z, h, x, l, 1 - c


def swap_lo(z, h, x, l, c):
    return z, h, x, 1 - l, c


def along_x(step):
    return lambda z, h, x, l, c: (z, h, (x + step) % NX, l, c)


def along_y(k):
    return lambda z, h, x, l, c: (z, h ^ (k // 2), x, l ^ (k % 2), c)


def turn(flip):
    def move(z, h, x, l, c):
        t = 2 * l + c
        return 2 * t + ((z % 2) ^ flip), h, x, z // 4, (z // 2) % 2

    return move


def nn(a, b):
    return jnp.dot(a, b, preferred_element_type=F32)


def tn(a, b):
    return lax.dot_general(a, b, (((0,), (0,)), ((), ())), preferred_element_type=F32)


def nt(a, b):
    return lax.dot_general(a, b, (((1,), (1,)), ((), ())), preferred_element_type=F32)


def shards(tokens, gate_weight, up_weight, down_weight, cotangent):
    dp, t = lax.axis_index("dp"), lax.axis_index("tensor")
    z, h, x = dp // (NH * NX), (dp // NX) % NH, dp % NX
    b = z % 2
    fb, hb = gate_weight.shape
    tb = tokens.shape[0]
    sub = tb // 4
    quarter = cotangent.shape[1]

    def picked(array, base, half):
        lanes = []
        for r in range(2):
            for j in range(NX):
                block = ((r ^ b) * NH + half) * NX + (x + j) % NX
                lanes.append(lax.dynamic_slice(array, (0, base + block * fb), (tb, fb)))
        wide = jnp.concatenate(lanes, axis=1)
        rows = []
        for oc in range(2):
            for ol in range(2):
                rows.append(lax.dynamic_slice(wide, ((t ^ (2 * ol + oc)) * sub, 0), (sub, wide.shape[1])))
        return jnp.concatenate(rows, axis=0)

    def placed(own, other):
        both = jnp.stack([own, other])
        rows = []
        for q in range(4):
            rel = q ^ t
            start = (rel % 2) * 2 + rel // 2
            rows.append(lax.dynamic_slice(both, (0, start * sub, 0), (2, sub, both.shape[2])))
        both = jnp.concatenate(rows, axis=1)
        lanes = []
        for p in range(2):
            for half in range(2):
                for s in range(NX):
                    block = (p ^ b) * NX + (s - x) % NX
                    lanes.append(lax.dynamic_slice(both, (half ^ h, 0, block * fb), (1, tb, fb))[0])
        return jnp.concatenate(lanes, axis=1)

    def joined(own, other):
        half = tb // 2
        return jnp.concatenate([own[:half], other[:half], own[half:], other[half:]], axis=0)

    def spread(block):
        everyone = lax.all_gather(block, "tensor", axis=0, tiled=False)
        column = jnp.stack([send(everyone, turn(0)), send(everyone, turn(1))])
        return [column] + [send(column, along_x(-j)) for j in range(1, NX)]

    gate_up = spread(jnp.stack([gate_weight, up_weight]))
    down = spread(down_weight)

    tok = joined(picked(tokens, t * quarter, h), send(picked(tokens, t * quarter, 1 - h), swap_hi))
    cot = joined(picked(cotangent, 0, h), send(picked(cotangent, 0, 1 - h), swap_hi))

    gu = jnp.stack(gate_up)
    gu = gu.transpose(3, 1, 0, 4, 2, 5).reshape(2, 2 * NX * fb, 4 * hb)
    dn = jnp.stack(down)
    dn = dn.transpose(2, 3, 1, 0, 4).reshape(4 * hb, 2 * NX * fb)

    def core_sum(part):
        rows = part.shape[0] // 2
        return part[:rows] + send(part[rows:], swap_core)

    def ring_sum(part):
        total = part[:sub]
        for k in range(1, 4):
            total = total + send(part[k * sub : (k + 1) * sub].astype(BF), along_y(k)).astype(F32)
        return total

    def ring_gather(block):
        four = jnp.concatenate([block] + [send(block, along_y(k)) for k in range(1, 4)], axis=0)
        return jnp.concatenate([four, send(four, swap_core)], axis=0)

    part = jnp.concatenate([nn(tok, gu[0]), nn(tok, gu[1])], axis=1)
    pre = ring_sum(core_sum(part))
    hid = 4 * hb
    gate_pre, up_pre = pre[:, :hid], pre[:, hid:]
    sig = jax.nn.sigmoid(gate_pre)
    act = gate_pre * sig
    hidden = ring_gather((act * up_pre).astype(BF))

    d_hidden = ring_sum(core_sum(nt(cot, dn)))
    d_gate = (d_hidden * up_pre * sig * (1.0 + gate_pre * (1.0 - sig))).astype(BF)
    d_up = (d_hidden * act).astype(BF)
    d_pair = ring_gather(jnp.concatenate([d_gate, d_up], axis=1))

    def output(wide):
        wide = wide.astype(BF)
        half = tb // 2
        own = jnp.concatenate([wide[:half], wide[2 * half : 3 * half]], axis=0)
        other = jnp.concatenate([wide[half : 2 * half], wide[3 * half :]], axis=0)
        return placed(own, send(other, swap_hi))

    layer_out = output(nn(hidden, dn))
    down_part = tn(hidden, cot)
    token_grad = output(nt(d_pair[:, :hid], gu[0]) + nt(d_pair[:, hid:], gu[1]))
    gu_part = tn(tok, d_pair)

    def collect(pieces):
        total = pieces[0]
        for j in range(1, NX):
            total = total + send(pieces[j].astype(BF), along_x(j)).astype(F32)
        total = total.astype(BF)
        total = send_back(total[0], turn(0)).astype(F32) + send_back(total[1], turn(1)).astype(F32)
        total = total.reshape(2, 2, *total.shape[1:])
        c, l = t % 2, t // 2
        mine = lax.dynamic_index_in_dim(total, c, 1, keepdims=False)
        yours = lax.dynamic_index_in_dim(total, 1 - c, 1, keepdims=False)
        total = mine + send(yours, swap_core)
        mine = lax.dynamic_index_in_dim(total, l, 0, keepdims=False)
        yours = lax.dynamic_index_in_dim(total, 1 - l, 0, keepdims=False)
        return mine + send(yours, swap_lo)

    down_pieces = down_part.reshape(4, hb, 2, NX, fb).transpose(3, 2, 0, 1, 4)
    gu_pieces = gu_part.reshape(2, NX, fb, 2, 4, hb).transpose(1, 0, 4, 3, 2, 5)
    down_grad = collect(down_pieces)
    gu_grad = collect(gu_pieces)
    return layer_out, token_grad, gu_grad[0], gu_grad[1], down_grad


def solution(mesh):
    placed = (
        P("dp", None),
        P("dp", "tensor"),
        P("dp", "tensor"),
        P("tensor", "dp"),
        P("dp", "tensor"),
    )
    return jax.shard_map(
        shards,
        mesh=mesh,
        in_specs=placed,
        out_specs=(
            P("dp", "tensor"),
            P("dp", "tensor"),
            P("dp", "tensor"),
            P("dp", "tensor"),
            P("tensor", "dp"),
        ),
        check_vma=False,
    )
```

```python
import functools

import jax
import jax.numpy as jnp
from jax import lax
from jax.experimental import pallas as pl
from jax.experimental.pallas import tpu as pltpu
from jax.sharding import PartitionSpec as P

NZ, NH, NX, NL, NC = 8, 2, 4, 2, 2
AXES = ("dp", "tensor")
BF = jnp.bfloat16
F32 = jnp.float32
VMEM_BYTES = 32 * 1024 * 1024


def index_of(z, h, x, l, c):
    return (((z * NH + h) * NX + x) * NL + l) * NC + c


def pairs_of(move):
    pairs = []
    for z in range(NZ):
        for h in range(NH):
            for x in range(NX):
                for l in range(NL):
                    for c in range(NC):
                        pairs.append((index_of(z, h, x, l, c), index_of(*move(z, h, x, l, c))))
    return pairs


def send(value, move):
    return lax.ppermute(value, AXES, pairs_of(move))


def send_back(value, move):
    return lax.ppermute(value, AXES, [(b, a) for a, b in pairs_of(move)])


def swap_hi(z, h, x, l, c):
    return z, 1 - h, x, l, c


def swap_core(z, h, x, l, c):
    return z, h, x, l, 1 - c


def along_x(step):
    return lambda z, h, x, l, c: (z, h, (x + step) % NX, l, c)


def along_y(k):
    return lambda z, h, x, l, c: (z, h ^ (k // 2), x, l ^ (k % 2), c)


def turn(f, g):
    def move(z, h, x, l, c):
        return 4 * ((z % 2) ^ f) + 2 * (l ^ g) + c, h, x, z // 4, (z // 2) % 2

    return move


TURNS = ((0, 0), (0, 1), (1, 0), (1, 1))


def nn(a, b):
    return jnp.dot(a, b, preferred_element_type=F32)


def tn(a, b):
    return lax.dot_general(a, b, (((0,), (0,)), ((), ())), preferred_element_type=F32)


def nt(a, b):
    return lax.dot_general(a, b, (((1,), (1,)), ((), ())), preferred_element_type=F32)


def call(body, shapes, args, flops=0):
    moved = sum(a.size * a.dtype.itemsize for a in args)
    moved += sum(functools.reduce(lambda p, q: p * q, s, 1) * jnp.dtype(d).itemsize for s, d in shapes)
    return pl.pallas_call(
        body,
        out_shape=[jax.ShapeDtypeStruct(s, d) for s, d in shapes],
        in_specs=[pl.BlockSpec(memory_space=pltpu.VMEM)] * len(args),
        out_specs=[pl.BlockSpec(memory_space=pltpu.VMEM)] * len(shapes),
        compiler_params=pltpu.CompilerParams(vmem_limit_bytes=VMEM_BYTES),
        cost_estimate=pl.CostEstimate(flops=flops, bytes_accessed=moved, transcendentals=0),
    )(*args)


def blocks_of(where, fb, sub):
    t, x, b = where[0], where[2], where[3]
    for oc in range(2):
        for ol in range(2):
            rows = pl.multiple_of((t ^ (2 * ol + oc)) * sub, sub)
            for r in range(2):
                for j in range(NX):
                    s = lax.rem(x + j, NX)

                    def lanes(half, r=r, s=s):
                        return pl.multiple_of((((r ^ b) * NH + half) * NX + s) * fb, fb)

                    yield (oc * 2 + ol) * sub, (r * NX + j) * fb, rows, lanes


def pick_body(where, tok, cot, tok_own, tok_oth, cot_own, cot_oth):
    sub = tok.shape[0] // 4
    fb = tok.shape[1] // 16
    h = where[1]
    for source, own, oth in ((tok, tok_own, tok_oth), (cot, cot_own, cot_oth)):
        for to_row, to_lane, row, lanes in blocks_of(where, fb, sub):
            own[to_row : to_row + sub, to_lane : to_lane + fb] = source[pl.ds(row, sub), pl.ds(lanes(h), fb)]
            oth[to_row : to_row + sub, to_lane : to_lane + fb] = source[pl.ds(row, sub), pl.ds(lanes(1 - h), fb)]


def place_body(where, own, oth, out):
    sub = own.shape[0] // 4
    fb = own.shape[1] // 8
    h = where[1]
    for at_row, at_lane, row, lanes in blocks_of(where, fb, sub):
        out[pl.ds(row, sub), pl.ds(lanes(h), fb)] = own[at_row : at_row + sub, at_lane : at_lane + fb]
        out[pl.ds(row, sub), pl.ds(lanes(1 - h), fb)] = oth[at_row : at_row + sub, at_lane : at_lane + fb]


def join(full, own, oth):
    tb = own.shape[0]
    half = tb // 2
    for oc in range(2):
        full[oc * tb : oc * tb + half, :] = own[oc * half : (oc + 1) * half, :]
        full[oc * tb + half : (oc + 1) * tb, :] = oth[oc * half : (oc + 1) * half, :]


def gate_up_body(own, oth, c0, c1, c2, c3, weights, full, keep, away):
    fb, hb = c0.shape[-2:]
    tb = own.shape[0]
    join(full, own, oth)
    for j, column in enumerate((c0, c1, c2, c3)):
        for f in range(2):
            row = (f * NX + j) * fb
            for m in range(2):
                for g in range(2):
                    for e in range(2):
                        lane = ((m * 2 + g) * 2 + e) * hb
                        weights[row : row + fb, lane : lane + hb] = column[f, g, e, m]
    away[...] = nn(full[tb:, :], weights[...]).astype(BF)
    keep[...] = nn(full[:tb, :], weights[...])


def down_body(own, oth, c0, c1, c2, c3, weights, full, keep, away):
    hb, fb = c0.shape[-2:]
    tb = own.shape[0]
    join(full, own, oth)
    for j, column in enumerate((c0, c1, c2, c3)):
        for f in range(2):
            lane = (f * NX + j) * fb
            for g in range(2):
                for e in range(2):
                    row = (g * 2 + e) * hb
                    weights[row : row + hb, lane : lane + fb] = column[f, g, e]
    away[...] = nt(full[tb:, :], weights[...]).astype(BF)
    keep[...] = nt(full[:tb, :], weights[...])


def down_grad_body(ha, hc, full, p0, p1, p2, p3):
    tb = ha.shape[0]
    hb, fb = p0.shape[-2:]
    for j, piece in ((1, p1), (3, p3), (2, p2), (0, p0)):
        for f in range(2):
            lane = (f * NX + j) * fb
            part = tn(ha[...], full[:tb, lane : lane + fb]) + tn(hc[...], full[tb:, lane : lane + fb])
            for g in range(2):
                for e in range(2):
                    row = (g * 2 + e) * hb
                    piece[f, g, e] = part[row : row + hb].astype(piece.dtype)


def gate_up_grad_body(da, dc, full, p0, p1, p2, p3):
    tb = da.shape[0]
    fb, hb = p0.shape[-2:]
    for j, piece in ((1, p1), (3, p3), (2, p2), (0, p0)):
        for f in range(2):
            lane = (f * NX + j) * fb
            part = tn(full[:tb, lane : lane + fb], da[...]) + tn(full[tb:, lane : lane + fb], dc[...])
            for m in range(2):
                for g in range(2):
                    for e in range(2):
                        at = ((m * 2 + g) * 2 + e) * hb
                        piece[f, g, e, m] = part[:, at : at + hb].astype(piece.dtype)


def part_rows(own, oth, oc, wide):
    half = wide.shape[0] // 2
    own[oc * half : (oc + 1) * half, :] = wide[:half].astype(BF)
    oth[oc * half : (oc + 1) * half, :] = wide[half:].astype(BF)


def layer_out_body(ha, hc, weights, own, oth):
    part_rows(own, oth, 0, nn(ha[...], weights[...]))
    part_rows(own, oth, 1, nn(hc[...], weights[...]))


def token_grad_body(da, dc, weights, own, oth):
    part_rows(own, oth, 0, nt(da[...], weights[...]))
    part_rows(own, oth, 1, nt(dc[...], weights[...]))


def shards(tokens, gate_weight, up_weight, down_weight, cotangent):
    dp, t = lax.axis_index("dp"), lax.axis_index("tensor")
    z, h, x = dp // (NH * NX), (dp // NX) % NH, dp % NX
    where = jnp.stack([t, h, x, z // 4]).astype(jnp.int32)
    fb, hb = gate_weight.shape
    tb = tokens.shape[0]
    sub = tb // 4
    quarter = cotangent.shape[1]
    wide, hid = 8 * fb, 4 * hb

    def pair(block):
        return jnp.stack([block, send(block, swap_core)])

    def column_of(both):
        four = [send(both, turn(f, g)) for f, g in TURNS]
        return jnp.stack(four).reshape(2, 2, *both.shape)

    def along(column):
        return [column] + [send(column, along_x(-j)) for j in range(1, NX)]

    gu_columns = along(column_of(pair(jnp.stack([gate_weight, up_weight]))))
    down_weight, _ = lax.optimization_barrier((down_weight, gu_columns[0]))
    down_column = column_of(pair(down_weight))
    down_column, gu_columns[1], gu_columns[3] = lax.optimization_barrier((down_column, gu_columns[1], gu_columns[3]))
    down_columns = along(down_column)

    rows = jax.ShapeDtypeStruct((tb, wide), BF)
    tok_own, tok_oth, cot_own, cot_oth = pl.pallas_call(
        pick_body,
        grid_spec=pltpu.PrefetchScalarGridSpec(
            num_scalar_prefetch=1,
            grid=(1,),
            in_specs=[
                pl.BlockSpec((tb, quarter), lambda i, where: (0, where[0])),
                pl.BlockSpec((tb, quarter), lambda i, where: (0, 0)),
            ],
            out_specs=[pl.BlockSpec((tb, wide), lambda i, where: (0, 0))] * 4,
        ),
        out_shape=[rows] * 4,
        compiler_params=pltpu.CompilerParams(vmem_limit_bytes=VMEM_BYTES),
        cost_estimate=pl.CostEstimate(flops=0, bytes_accessed=8 * tb * wide * 2, transcendentals=0),
    )(where, tokens, cotangent)
    tok_far = send(tok_oth, swap_hi)
    cot_far = send(cot_oth, swap_hi)

    def placed(own, far):
        return pl.pallas_call(
            place_body,
            grid_spec=pltpu.PrefetchScalarGridSpec(
                num_scalar_prefetch=1,
                grid=(1,),
                in_specs=[pl.BlockSpec((tb, wide), lambda i, where: (0, 0))] * 2,
                out_specs=pl.BlockSpec((tb, quarter), lambda i, where: (0, 0)),
            ),
            out_shape=jax.ShapeDtypeStruct((tb, quarter), BF),
            compiler_params=pltpu.CompilerParams(vmem_limit_bytes=VMEM_BYTES),
            cost_estimate=pl.CostEstimate(flops=0, bytes_accessed=4 * tb * wide * 2, transcendentals=0),
        )(where, own, far)

    def ring_sum(keep, away):
        part = keep + send(away, swap_core).astype(F32)
        total = part[:sub]
        for k in range(1, 4):
            total = total + send(part[k * sub : (k + 1) * sub].astype(BF), along_y(k)).astype(F32)
        return total

    def ring_gather(block):
        four = jnp.concatenate([block] + [send(block, along_y(k)) for k in range(1, 4)], axis=0)
        return four, send(four, swap_core)

    product = 2 * 2 * tb * wide * hid
    gu_weights, tok, keep, away = call(
        gate_up_body,
        [((wide, 2 * hid), BF), ((2 * tb, wide), BF), ((tb, 2 * hid), F32), ((tb, 2 * hid), BF)],
        [tok_own, tok_far, *gu_columns],
        2 * product,
    )
    pre = ring_sum(keep, away)
    gate_pre, up_pre = pre[:, :hid], pre[:, hid:]
    sig = jax.nn.sigmoid(gate_pre)
    act = gate_pre * sig
    hidden = ring_gather((act * up_pre).astype(BF))

    down_weights, cot, keep, away = call(
        down_body,
        [((hid, wide), BF), ((2 * tb, wide), BF), ((tb, hid), F32), ((tb, hid), BF)],
        [cot_own, cot_far, *down_columns],
        product,
    )
    d_hidden = ring_sum(keep, away)
    d_gate = (d_hidden * up_pre * sig * (1.0 + gate_pre * (1.0 - sig))).astype(BF)
    d_up = (d_hidden * act).astype(BF)
    d_pair = ring_gather(jnp.concatenate([d_gate, d_up], axis=1))

    def collect(pieces):
        total = pieces[0]
        for j in range(1, NX):
            total = total + send(pieces[j], along_x(j)).astype(F32)
        total = total.astype(BF)
        total = sum(send_back(total[f, g], turn(f, g)).astype(F32) for f, g in TURNS)
        return total[0] + send(total[1], swap_core)

    def output(body, both, weights, flops):
        own, oth = call(body, [((tb, wide), BF)] * 2, [*both, weights], flops)
        return placed(own, send(oth, swap_hi))

    shape = (2, 2, 2, hb, fb)
    down_pieces = call(down_grad_body, [(shape, F32)] + [(shape, BF)] * 3, [*hidden, cot], product)
    layer_out = output(layer_out_body, hidden, down_weights, product)
    down_grad = collect(down_pieces)
    shape = (2, 2, 2, 2, fb, hb)
    gu_pieces = call(gate_up_grad_body, [(shape, F32)] + [(shape, BF)] * 3, [*d_pair, tok], 2 * product)
    gu_grad = collect(gu_pieces)
    token_grad = output(token_grad_body, d_pair, gu_weights, 2 * product)
    return layer_out, token_grad, gu_grad[0], gu_grad[1], down_grad


def solution(mesh):
    placed = (
        P("dp", None),
        P("dp", "tensor"),
        P("dp", "tensor"),
        P("tensor", "dp"),
        P("dp", "tensor"),
    )
    return jax.shard_map(
        shards,
        mesh=mesh,
        in_specs=placed,
        out_specs=(
            P("dp", "tensor"),
            P("dp", "tensor"),
            P("dp", "tensor"),
            P("dp", "tensor"),
            P("tensor", "dp"),
        ),
        check_vma=False,
    )
```

```python
import functools

import jax
import jax.numpy as jnp
from jax import lax
from jax.experimental import pallas as pl
from jax.experimental.pallas import tpu as pltpu
from jax.sharding import PartitionSpec as P

NZ, NH, NX, NL, NC = 8, 2, 4, 2, 2
AXES = ("dp", "tensor")
BF = jnp.bfloat16
F32 = jnp.float32
VMEM_BYTES = 32 * 1024 * 1024


def index_of(z, h, x, l, c):
    return (((z * NH + h) * NX + x) * NL + l) * NC + c


def pairs_of(move):
    pairs = []
    for z in range(NZ):
        for h in range(NH):
            for x in range(NX):
                for l in range(NL):
                    for c in range(NC):
                        pairs.append((index_of(z, h, x, l, c), index_of(*move(z, h, x, l, c))))
    return pairs


def send(value, move):
    return lax.ppermute(value, AXES, pairs_of(move))


def send_back(value, move):
    return lax.ppermute(value, AXES, [(b, a) for a, b in pairs_of(move)])


def swap_hi(z, h, x, l, c):
    return z, 1 - h, x, l, c


def swap_core(z, h, x, l, c):
    return z, h, x, l, 1 - c


def along_x(step):
    return lambda z, h, x, l, c: (z, h, (x + step) % NX, l, c)


def along_y(k):
    return lambda z, h, x, l, c: (z, h ^ (k // 2), x, l ^ (k % 2), c)


def turn(f, g):
    def move(z, h, x, l, c):
        return 4 * ((z % 2) ^ f) + 2 * (l ^ g) + c, h, x, z // 4, (z // 2) % 2

    return move


PARTNERS = [[(z * NH + h) * NX + x for h in range(NH)] for z in range(NZ) for x in range(NX)]


def nn(a, b):
    return jnp.dot(a, b, preferred_element_type=F32)


def tn(a, b):
    return lax.dot_general(a, b, (((0,), (0,)), ((), ())), preferred_element_type=F32)


def nt(a, b):
    return lax.dot_general(a, b, (((1,), (1,)), ((), ())), preferred_element_type=F32)


def call(body, shapes, args, flops=0):
    moved = sum(a.size * a.dtype.itemsize for a in args)
    moved += sum(functools.reduce(lambda p, q: p * q, s, 1) * jnp.dtype(d).itemsize for s, d in shapes)
    return pl.pallas_call(
        body,
        out_shape=[jax.ShapeDtypeStruct(s, d) for s, d in shapes],
        in_specs=[pl.BlockSpec(memory_space=pltpu.VMEM)] * len(args),
        out_specs=[pl.BlockSpec(memory_space=pltpu.VMEM)] * len(shapes),
        compiler_params=pltpu.CompilerParams(vmem_limit_bytes=VMEM_BYTES),
        cost_estimate=pl.CostEstimate(flops=flops, bytes_accessed=moved, transcendentals=0),
    )(*args)


def call_at(body, where, args, shapes, flops=0):
    def at(block, shifted):
        zeros = (0,) * (len(block) - 1)
        return pl.BlockSpec(block, lambda i, where: (*zeros, where[0] if shifted else 0))

    moved = sum(functools.reduce(lambda p, q: p * q, b, 1) * 2 for _, b, _ in args)
    moved += sum(functools.reduce(lambda p, q: p * q, s, 1) * jnp.dtype(d).itemsize for s, d in shapes)
    return pl.pallas_call(
        body,
        grid_spec=pltpu.PrefetchScalarGridSpec(
            num_scalar_prefetch=1,
            grid=(1,),
            in_specs=[at(block, shifted) for _, block, shifted in args],
            out_specs=[at(shape, False) for shape, _ in shapes],
        ),
        out_shape=[jax.ShapeDtypeStruct(s, d) for s, d in shapes],
        compiler_params=pltpu.CompilerParams(vmem_limit_bytes=VMEM_BYTES),
        cost_estimate=pl.CostEstimate(flops=flops, bytes_accessed=moved, transcendentals=0),
    )(where, *[a for a, _, _ in args])


def blocks_of(where, fb, sub):
    t, x, b = where[0], where[2], where[3]
    for oc in range(2):
        for ol in range(2):
            rows = pl.multiple_of((t ^ (2 * ol + oc)) * sub, sub)
            for r in range(2):
                for j in range(NX):
                    s = lax.rem(x + j, NX)

                    def lanes(half, r=r, s=s):
                        return pl.multiple_of((((r ^ b) * NH + half) * NX + s) * fb, fb)

                    yield (oc * 2 + ol) * sub, (r * NX + j) * fb, rows, lanes


def pick_body(where, tok, cot, own, oth):
    sub = tok.shape[0] // 4
    fb = tok.shape[1] // 16
    h = where[1]
    for m, source in enumerate((tok, cot)):
        for to_row, to_lane, row, lanes in blocks_of(where, fb, sub):
            oth[m, to_row : to_row + sub, to_lane : to_lane + fb] = source[pl.ds(row, sub), pl.ds(lanes(1 - h), fb)]
            own[m, to_row : to_row + sub, to_lane : to_lane + fb] = source[pl.ds(row, sub), pl.ds(lanes(h), fb)]


def place_body(where, own, both, layer_out, token_grad):
    sub = own.shape[1] // 4
    fb = own.shape[2] // 8
    h = where[1]
    for m, out in enumerate((layer_out, token_grad)):
        for at_row, at_lane, row, lanes in blocks_of(where, fb, sub):
            out[pl.ds(row, sub), pl.ds(lanes(h), fb)] = own[m, at_row : at_row + sub, at_lane : at_lane + fb]
            out[pl.ds(row, sub), pl.ds(lanes(1 - h), fb)] = both[1 - h, m, at_row : at_row + sub, at_lane : at_lane + fb]


def forward_body(where, own, both, *refs):
    columns, (gu, dn, tok, cot, keep, away) = refs[:8], refs[8:]
    fb = columns[0].shape[-1]
    tb = own.shape[1]
    half = tb // 2
    h = where[1]
    for m, full in enumerate((tok, cot)):
        for oc in range(2):
            full[oc * tb : oc * tb + half, :] = own[m, oc * half : (oc + 1) * half, :]
            full[oc * tb + half : (oc + 1) * tb, :] = both[1 - h, m, oc * half : (oc + 1) * half, :]
    for f in range(2):
        for j in range(NX):
            column = columns[f * NX + j]
            at = (f * NX + j) * fb
            for g in range(2):
                for e in range(2):
                    unit = (g * 2 + e) * fb
                    gu[at : at + fb, unit : unit + fb] = column[g, e, 0]
                    gu[at : at + fb, 4 * fb + unit : 4 * fb + unit + fb] = column[g, e, 1]
                    dn[unit : unit + fb, at : at + fb] = column[g, e, 2]
    wide = gu.shape[1]
    away[:, :wide] = nn(tok[tb:, :], gu[...]).astype(BF)
    away[:, wide:] = nt(cot[tb:, :], dn[...]).astype(BF)
    keep[:, :wide] = nn(tok[:tb, :], gu[...])
    keep[:, wide:] = nt(cot[:tb, :], dn[...])


def grad_body(f, da, dc, tok, cot, p1, p3, p2, p0):
    tb = da.shape[0]
    fb = p0.shape[-1]
    hid = 4 * fb
    for j, piece in ((1, p1), (3, p3), (2, p2), (0, p0)):
        at = (f * NX + j) * fb
        gu = tn(tok[:tb, at : at + fb], da[:, : 2 * hid]) + tn(tok[tb:, at : at + fb], dc[:, : 2 * hid])
        dn = tn(da[:, 2 * hid :], cot[:tb, at : at + fb]) + tn(dc[:, 2 * hid :], cot[tb:, at : at + fb])
        for g in range(2):
            for e in range(2):
                unit = (g * 2 + e) * fb
                piece[g, e, 0] = gu[:, unit : unit + fb].astype(piece.dtype)
                piece[g, e, 1] = gu[:, hid + unit : hid + unit + fb].astype(piece.dtype)
                piece[g, e, 2] = dn[unit : unit + fb].astype(piece.dtype)


def output_body(da, dc, gu, dn, own, oth):
    tb, wide = da.shape[0], gu.shape[1]
    half = tb // 2
    for oc, part in ((0, da), (1, dc)):
        out = nn(part[:, wide:], dn[...]).astype(BF)
        grad = nt(part[:, :wide], gu[...]).astype(BF)
        for m, rows in ((0, out), (1, grad)):
            own[m, oc * half : (oc + 1) * half, :] = rows[:half]
            oth[m, oc * half : (oc + 1) * half, :] = rows[half:]


def shards(tokens, gate_weight, up_weight, down_weight, cotangent):
    dp, t = lax.axis_index("dp"), lax.axis_index("tensor")
    z, h, x = dp // (NH * NX), (dp // NX) % NH, dp % NX
    where = jnp.stack([t, h, x, z // 4]).astype(jnp.int32)
    fb = gate_weight.shape[0]
    tb = tokens.shape[0]
    sub = tb // 4
    quarter = cotangent.shape[1]
    wide, hid = 8 * fb, 4 * fb

    own, oth = call_at(
        pick_body,
        where,
        [(tokens, (tb, quarter), True), (cotangent, (tb, quarter), False)],
        [((2, tb, wide), BF)] * 2,
    )
    both = lax.all_gather(oth, "dp", axis_index_groups=PARTNERS)

    block = jnp.stack([gate_weight, up_weight, down_weight])
    pair = jnp.stack([block, send(block, swap_core)])

    def column_of(f, value):
        return [send(value, turn(f, g)) for g in range(2)]

    def along(column):
        return [column] + [send(column, along_x(-j)) for j in range(1, NX)]

    near = column_of(0, pair)
    pair, *near = lax.optimization_barrier((pair, *near))
    near = along(jnp.stack(near))
    far = along(jnp.stack(column_of(1, pair)))

    product = 2 * 2 * tb * wide * hid
    gu, dn, tok, cot, keep, away = call_at(
        forward_body,
        where,
        [(a, a.shape, False) for a in (own, both, *near, *far)],
        [((wide, 2 * hid), BF), ((hid, wide), BF), ((2 * tb, wide), BF), ((2 * tb, wide), BF), ((tb, 3 * hid), F32), ((tb, 3 * hid), BF)],
        3 * product,
    )
    part = keep + send(away, swap_core).astype(F32)
    pre = part[:sub]
    for k in range(1, 4):
        pre = pre + send(part[k * sub : (k + 1) * sub].astype(BF), along_y(k)).astype(F32)
    gate_pre, up_pre, d_hidden = pre[:, :hid], pre[:, hid : 2 * hid], pre[:, 2 * hid :]
    sig = jax.nn.sigmoid(gate_pre)
    act = gate_pre * sig
    hidden = (act * up_pre).astype(BF)
    d_gate = (d_hidden * up_pre * sig * (1.0 + gate_pre * (1.0 - sig))).astype(BF)
    d_up = (d_hidden * act).astype(BF)
    mine = jnp.concatenate([d_gate, d_up, hidden], axis=1)
    four = jnp.concatenate([mine] + [send(mine, along_y(k)) for k in range(1, 4)], axis=0)
    terms = (four, send(four, swap_core))

    shape = (2, 2, 3, fb, fb)

    def pieces_of(f):
        return call(functools.partial(grad_body, f), [(shape, BF)] * 3 + [(shape, F32)], [*terms, tok, cot], 3 * product // 2)

    def summed(moved, kept):
        total = kept
        for piece in moved:
            total = total + piece.astype(F32)
        return total.astype(BF)

    def returned(f, total):
        return [send_back(total[g], turn(f, g)) for g in range(2)]

    p1, p3, p2, p0 = pieces_of(0)
    q1, q3, q2, q0 = pieces_of(1)
    p1, p3, p2 = send(p1, along_x(1)), send(p3, along_x(3)), send(p2, along_x(2))
    p1, p3, q1, q3, q2 = lax.optimization_barrier((p1, p3, q1, q3, q2))
    back = returned(0, summed((p1, p3, p2), p0))
    q1, q3, q2 = send(q1, along_x(1)), send(q3, along_x(3)), send(q2, along_x(2))

    own, oth = call(output_body, [((2, tb, wide), BF)] * 2, [*terms, gu, dn], 3 * product)
    both = lax.all_gather(oth, "dp", axis_index_groups=PARTNERS)
    layer_out, token_grad = call_at(
        place_body,
        where,
        [(own, own.shape, False), (both, both.shape, False)],
        [((tb, quarter), BF)] * 2,
    )

    back = back + returned(1, summed((q1, q3, q2), q0))
    total = sum(piece.astype(F32) for piece in back)
    kept, moved, layer_out, token_grad = lax.optimization_barrier((total[0], total[1], layer_out, token_grad))
    total = kept + send(moved, swap_core)
    return layer_out, token_grad, total[0], total[1], total[2]


def solution(mesh):
    placed = (
        P("dp", None),
        P("dp", "tensor"),
        P("dp", "tensor"),
        P("tensor", "dp"),
        P("dp", "tensor"),
    )
    return jax.shard_map(
        shards,
        mesh=mesh,
        in_specs=placed,
        out_specs=(
            P("dp", "tensor"),
            P("dp", "tensor"),
            P("dp", "tensor"),
            P("dp", "tensor"),
            P("tensor", "dp"),
        ),
        check_vma=False,
    )
```

```python
import functools

import jax
import jax.numpy as jnp
from jax import lax
from jax.experimental import pallas as pl
from jax.experimental.pallas import tpu as pltpu
from jax.sharding import PartitionSpec as P

NZ, NH, NX, NL, NC = 8, 2, 4, 2, 2
AXES = ("dp", "tensor")
BF = jnp.bfloat16
F32 = jnp.float32
VMEM_BYTES = 32 * 1024 * 1024


def index_of(z, h, x, l, c):
    return (((z * NH + h) * NX + x) * NL + l) * NC + c


def pairs_of(move):
    pairs = []
    for z in range(NZ):
        for h in range(NH):
            for x in range(NX):
                for l in range(NL):
                    for c in range(NC):
                        pairs.append((index_of(z, h, x, l, c), index_of(*move(z, h, x, l, c))))
    return pairs


def send(value, move):
    return lax.ppermute(value, AXES, pairs_of(move))


def send_back(value, move):
    return lax.ppermute(value, AXES, [(b, a) for a, b in pairs_of(move)])


def swap_hi(z, h, x, l, c):
    return z, 1 - h, x, l, c


def swap_core(z, h, x, l, c):
    return z, h, x, l, 1 - c


def along_x(step):
    return lambda z, h, x, l, c: (z, h, (x + step) % NX, l, c)


def turn(f, g):
    def move(z, h, x, l, c):
        return 4 * ((z % 2) ^ f) + 2 * (l ^ g) + c, h, x, z // 4, (z // 2) % 2

    return move


def after(value, *others):
    return lax.optimization_barrier((value, *others))[0]


def along_y(k):
    return lambda z, h, x, l, c: (z, h ^ (k // 2), x, l ^ (k % 2), c)


RING = [[index_of(z, h, x, l, c) for h in range(NH) for l in range(NL) for c in range(NC)] for z in range(NZ) for x in range(NX)]


def nn(a, b):
    return jnp.dot(a, b, preferred_element_type=F32)


def tn(a, b):
    return lax.dot_general(a, b, (((0,), (0,)), ((), ())), preferred_element_type=F32)


def nt(a, b):
    return lax.dot_general(a, b, (((1,), (1,)), ((), ())), preferred_element_type=F32)


def call(body, shapes, args, flops=0, where=None):
    moved = sum(a.size * a.dtype.itemsize for a in args)
    moved += sum(functools.reduce(lambda p, q: p * q, s, 1) * jnp.dtype(d).itemsize for s, d in shapes)
    scalars = [] if where is None else [where]
    return pl.pallas_call(
        body,
        out_shape=[jax.ShapeDtypeStruct(s, d) for s, d in shapes],
        in_specs=[pl.BlockSpec(memory_space=pltpu.SMEM)] * len(scalars) + [pl.BlockSpec(memory_space=pltpu.VMEM)] * len(args),
        out_specs=[pl.BlockSpec(memory_space=pltpu.VMEM)] * len(shapes),
        compiler_params=pltpu.CompilerParams(vmem_limit_bytes=VMEM_BYTES),
        cost_estimate=pl.CostEstimate(flops=flops, bytes_accessed=moved, transcendentals=0),
    )(*scalars, *args)


def blocks_of(where, fb):
    x, b = where[1], where[2]
    for r in range(2):
        for j in range(NX):
            s = lax.rem(x + j, NX)

            def lanes(half, r=r, s=s):
                return pl.multiple_of((((r ^ b) * NH + half) * NX + s) * fb, fb)

            yield (r * NX + j) * fb, lanes


def pick_body(where, tok, cot, own, oth):
    fb = tok.shape[1] // 16
    h = where[0]
    for m, source in enumerate((tok, cot)):
        for at, lanes in blocks_of(where, fb):
            oth[m, :, at : at + fb] = source[:, pl.ds(lanes(1 - h), fb)]
            own[m, :, at : at + fb] = source[:, pl.ds(lanes(h), fb)]


def place_body(where, own, far, layer_out, token_grad):
    fb = own.shape[2] // 8
    h = where[0]
    for m, out in enumerate((layer_out, token_grad)):
        for at, lanes in blocks_of(where, fb):
            out[:, pl.ds(lanes(h), fb)] = own[m, :, at : at + fb]
            out[:, pl.ds(lanes(1 - h), fb)] = far[m, :, at : at + fb]


def join_body(where, own, far, tok, cot):
    tb = own.shape[1]
    h = where[0]
    for m, full in enumerate((tok, cot)):
        full[pl.ds(pl.multiple_of(h * tb, tb), tb), :] = own[m]
        full[pl.ds(pl.multiple_of((1 - h) * tb, tb), tb), :] = far[m]


def forward_body(tok, cot, c0, c1, c2, c3, gu, dn, part):
    fb = c0.shape[-1]
    for f in range(2):
        for j, column in enumerate((c0, c1, c2, c3)):
            at = (f * NX + j) * fb
            for e in range(2):
                gu[at : at + fb, e * fb : e * fb + fb] = column[f, e, 0]
                gu[at : at + fb, (2 + e) * fb : (2 + e) * fb + fb] = column[f, e, 1]
                dn[e * fb : e * fb + fb, at : at + fb] = column[f, e, 2]
    wide = gu.shape[1]
    part[:, :wide] = nn(tok[...], gu[...]).astype(BF)
    part[:, wide:] = nt(cot[...], dn[...]).astype(BF)


def ordered_body(where, mine, twin, tok, cot, d, p1, p3, p2, p0):
    sub = mine.shape[0] // 4
    h, l, c = where[0], where[3], where[4]
    for k in range(4):
        for flip, part in ((0, mine), (1, twin)):
            row = (((h ^ (k // 2)) * NL + (l ^ (k % 2))) * NC + (c ^ flip)) * sub
            d[pl.ds(pl.multiple_of(row, sub), sub), :] = part[k * sub : (k + 1) * sub, :]
    grad_body(d, tok, cot, p1, p3, p2, p0)


def grad_body(d, tok, cot, p1, p3, p2, p0):
    fb = p0.shape[-1]
    wide = 4 * fb
    for j, piece in ((1, p1), (3, p3), (2, p2), (0, p0)):
        for f in range(2):
            at = (f * NX + j) * fb
            gu = tn(tok[:, at : at + fb], d[:, :wide])
            dn = tn(d[:, wide:], cot[:, at : at + fb])
            for e in range(2):
                piece[f, e, 0] = gu[:, e * fb : e * fb + fb].astype(piece.dtype)
                piece[f, e, 1] = gu[:, (2 + e) * fb : (2 + e) * fb + fb].astype(piece.dtype)
                piece[f, e, 2] = dn[e * fb : e * fb + fb].astype(piece.dtype)


def output_body(where, d, e, gu_d, dn_d, gu_e, dn_e, own, oth):
    wide = gu_d.shape[1]
    tb = own.shape[1]
    h = where[0]
    for half, to in ((h, own), (1 - h, oth)):
        rows = pl.ds(pl.multiple_of(half * tb, tb), tb)
        to[0] = (nn(d[rows, wide:], dn_d[...]) + nn(e[rows, wide:], dn_e[...])).astype(BF)
        to[1] = (nt(d[rows, :wide], gu_d[...]) + nt(e[rows, :wide], gu_e[...])).astype(BF)


def shards(tokens, gate_weight, up_weight, down_weight, cotangent):
    dp, t = lax.axis_index("dp"), lax.axis_index("tensor")
    z, h, x = dp // (NH * NX), (dp // NX) % NH, dp % NX
    where = jnp.stack([h, x, z // 4, t // 2, t % 2]).astype(jnp.int32)
    fb = gate_weight.shape[0]
    tb = tokens.shape[0]
    quarter = cotangent.shape[1]
    wide, unit = 8 * fb, 2 * fb

    with jax.named_scope("weights_core"):
        block = jnp.stack([gate_weight, up_weight, down_weight])
        pair = jnp.stack([block, send(block, swap_core)])

    def turned(g, value):
        with jax.named_scope(f"weights_turn_{g}"):
            return [send(value, turn(f, g)) for f in range(2)]

    def along(g, column):
        with jax.named_scope(f"weights_x_{g}"):
            return [column] + [send(column, along_x(-j)) for j in range(1, NX)]

    first = turned(0, pair)
    where, tokens, cotangent, _ = lax.optimization_barrier((where, tokens, cotangent, pair))
    picked = lax.dynamic_slice(tokens, (0, t * quarter), (tb, quarter))
    with jax.named_scope("pick"):
        own, oth = call(pick_body, [((2, tb, wide), BF)] * 2, [picked, cotangent], 0, where)
    with jax.named_scope("input_swap"):
        far = send(oth, swap_hi)
    with jax.named_scope("join"):
        tok, cot = call(join_body, [((2 * tb, wide), BF)] * 2, [own, far], 0, where)
    pair, *first = lax.optimization_barrier((pair, *first))
    first = along(0, jnp.stack(first))
    second = jnp.stack(turned(1, after(pair, far)))
    first[0] = after(first[0], second)
    second = along(1, after(second, first[1], first[2], first[3]))

    product = 2 * 2 * tb * wide * unit

    def forward(g, columns, rows):
        with jax.named_scope(f"forward_{g}"):
            return call(
                forward_body,
                [((wide, 2 * unit), BF), ((unit, wide), BF), ((2 * tb, 3 * unit), BF)],
                [rows, cot, *columns],
                3 * product,
            )

    def reduced(g, part):
        with jax.named_scope(f"reduce_ring_{g}"):
            parts = lax.all_to_all(part.reshape(8, -1, part.shape[1]), AXES, 0, 0, axis_index_groups=RING, tiled=True)
            return jnp.sum(parts.astype(F32), axis=0)

    def activations(pre):
        gate_pre, up_pre, d_hidden = pre[:, :unit], pre[:, unit : 2 * unit], pre[:, 2 * unit :]
        sig = jax.nn.sigmoid(gate_pre)
        act = gate_pre * sig
        hidden = (act * up_pre).astype(BF)
        d_gate = (d_hidden * up_pre * sig * (1.0 + gate_pre * (1.0 - sig))).astype(BF)
        d_up = (d_hidden * act).astype(BF)
        return jnp.concatenate([d_gate, d_up, hidden], axis=1)

    def gathered(g, mine):
        with jax.named_scope(f"gather_ring_{g}"):
            four = jnp.concatenate([mine] + [send(mine, along_y(k)) for k in range(1, 4)], axis=0)
        with jax.named_scope(f"gather_core_{g}"):
            return four, send(four, swap_core)

    def gathered_at_once(g, mine):
        with jax.named_scope(f"gather_ring_{g}"):
            copies = jnp.broadcast_to(mine, (8, *mine.shape))
            return (lax.all_to_all(copies, AXES, 0, 0, axis_index_groups=RING, tiled=True).reshape(-1, mine.shape[1]),)

    shape = (2, 2, 3, fb, fb)

    def pieces_of(g, terms):
        shapes = [(shape, BF)] * 3 + [(shape, F32)]
        with jax.named_scope(f"grads_{g}"):
            if len(terms) == 1:
                return [*terms, *call(grad_body, shapes, [*terms, tok, cot], 3 * product)]
            return call(ordered_body, [((2 * tb, 3 * unit), BF)] + shapes, [*terms, tok, cot], 3 * product, where)

    def summed(moved, kept):
        total = kept
        for piece in moved:
            total = total + piece.astype(F32)
        return total.astype(BF)

    def returned(g, total):
        with jax.named_scope(f"grads_turn_{g}"):
            return [send_back(total[f], turn(f, g)) for f in range(2)]

    gu_0, dn_0, part_0 = forward(0, first, tok)
    mine_0 = activations(reduced(0, part_0))
    gu_1, dn_1, part_1 = forward(1, second, after(tok, mine_0))
    terms_0 = gathered(0, mine_0)
    d_0, p1, p3, p2, p0 = pieces_of(0, terms_0)
    with jax.named_scope("grads_x_0"):
        p1, p3, p2 = send(p1, along_x(1)), send(p3, along_x(3)), send(p2, along_x(2))

    terms_1 = gathered_at_once(1, after(activations(reduced(1, part_1)), d_0))
    d_1, q1, q3, q2, q0 = pieces_of(1, terms_1)
    with jax.named_scope("outputs"):
        own, oth = call(output_body, [((2, tb, wide), BF)] * 2, [d_0, d_1, gu_0, dn_0, gu_1, dn_1], 6 * product, where)
    p1, p3, q1, q3, q2, oth = lax.optimization_barrier((p1, p3, q1, q3, q2, oth))
    back = returned(0, summed((p1, p3, p2), p0))
    with jax.named_scope("grads_x_1"):
        q1, q3, q2 = send(q1, along_x(1)), send(q3, along_x(3)), send(q2, along_x(2))

    with jax.named_scope("output_swap"):
        far = send(oth, swap_hi)
    with jax.named_scope("place"):
        layer_out, token_grad = call(place_body, [((tb, quarter), BF)] * 2, [own, far], 0, where)

    back = back + returned(1, after(summed((q1, q3, q2), q0), far))
    total = sum(piece.astype(F32) for piece in back)
    kept, moved, layer_out, token_grad = lax.optimization_barrier((total[0], total[1], layer_out, token_grad))
    with jax.named_scope("grads_core"):
        total = kept + send(moved, swap_core)
    return layer_out, token_grad, total[0], total[1], total[2]


def solution(mesh):
    placed = (
        P("dp", None),
        P("dp", "tensor"),
        P("dp", "tensor"),
        P("tensor", "dp"),
        P("dp", "tensor"),
    )
    return jax.shard_map(
        shards,
        mesh=mesh,
        in_specs=placed,
        out_specs=(
            P("dp", "tensor"),
            P("dp", "tensor"),
            P("dp", "tensor"),
            P("dp", "tensor"),
            P("tensor", "dp"),
        ),
        check_vma=False,
    )
```

```python
import functools

import jax
import jax.numpy as jnp
from jax import lax
from jax.experimental import pallas as pl
from jax.experimental.pallas import tpu as pltpu
from jax.sharding import PartitionSpec as P

NZ, NH, NX, NL, NC = 8, 2, 4, 2, 2
AXES = ("dp", "tensor")
BF = jnp.bfloat16
F32 = jnp.float32
VMEM_BYTES = 16 * 1024 * 1024


def index_of(z, h, x, l, c):
    return (((z * NH + h) * NX + x) * NL + l) * NC + c


def pairs_of(move):
    pairs = []
    for z in range(NZ):
        for h in range(NH):
            for x in range(NX):
                for l in range(NL):
                    for c in range(NC):
                        pairs.append((index_of(z, h, x, l, c), index_of(*move(z, h, x, l, c))))
    return pairs


def send(value, move):
    return lax.ppermute(value, AXES, pairs_of(move))


def send_back(value, move):
    return lax.ppermute(value, AXES, [(b, a) for a, b in pairs_of(move)])


def swap_hi(z, h, x, l, c):
    return z, 1 - h, x, l, c


def swap_core(z, h, x, l, c):
    return z, h, x, l, 1 - c


def along_x(step):
    return lambda z, h, x, l, c: (z, h, (x + step) % NX, l, c)


def along_y(k):
    return lambda z, h, x, l, c: (z, h ^ (k // 2), x, l ^ (k % 2), c)


def turn(f, g):
    def move(z, h, x, l, c):
        return 4 * ((z % 2) ^ f) + 2 * (l ^ g) + c, h, x, z // 4, (z // 2) % 2

    return move


def after(value, *others):
    return lax.optimization_barrier((value, *others))[0]


def nn(a, b):
    return jnp.dot(a, b, preferred_element_type=F32)


def tn(a, b):
    return lax.dot_general(a, b, (((0,), (0,)), ((), ())), preferred_element_type=F32)


def nt(a, b):
    return lax.dot_general(a, b, (((1,), (1,)), ((), ())), preferred_element_type=F32)


def call(body, shapes, args, flops=0, where=None):
    moved = sum(a.size * a.dtype.itemsize for a in args)
    moved += sum(functools.reduce(lambda p, q: p * q, s, 1) * jnp.dtype(d).itemsize for s, d in shapes)
    scalars = [] if where is None else [where]
    return pl.pallas_call(
        body,
        out_shape=[jax.ShapeDtypeStruct(s, d) for s, d in shapes],
        in_specs=[pl.BlockSpec(memory_space=pltpu.SMEM)] * len(scalars) + [pl.BlockSpec(memory_space=pltpu.VMEM)] * len(args),
        out_specs=[pl.BlockSpec(memory_space=pltpu.VMEM)] * len(shapes),
        compiler_params=pltpu.CompilerParams(vmem_limit_bytes=VMEM_BYTES),
        cost_estimate=pl.CostEstimate(flops=flops, bytes_accessed=moved, transcendentals=0),
    )(*scalars, *args)


def blocks_of(where, fb, sub):
    t, x, b = where[0], where[2], where[3]
    for oc in range(2):
        for ol in range(2):
            rows = pl.multiple_of((t ^ (2 * ol + oc)) * sub, sub)
            for r in range(2):
                for j in range(NX):
                    s = lax.rem(x + j, NX)

                    def lanes(half, r=r, s=s):
                        return pl.multiple_of((((r ^ b) * NH + half) * NX + s) * fb, fb)

                    yield (oc * 2 + ol) * sub, (r * NX + j) * fb, rows, lanes


def pick_body(where, tok, cot, own, oth):
    sub = tok.shape[0] // 4
    fb = tok.shape[1] // 16
    h = where[1]
    for m, source in enumerate((tok, cot)):
        for to_row, to_lane, row, lanes in blocks_of(where, fb, sub):
            oth[m, to_row : to_row + sub, to_lane : to_lane + fb] = source[pl.ds(row, sub), pl.ds(lanes(1 - h), fb)]
            own[m, to_row : to_row + sub, to_lane : to_lane + fb] = source[pl.ds(row, sub), pl.ds(lanes(h), fb)]


def place_body(where, own, far, layer_out, token_grad):
    sub = own.shape[1] // 4
    fb = own.shape[2] // 8
    h = where[1]
    for m, out in enumerate((layer_out, token_grad)):
        for at_row, at_lane, row, lanes in blocks_of(where, fb, sub):
            out[pl.ds(row, sub), pl.ds(lanes(h), fb)] = own[m, at_row : at_row + sub, at_lane : at_lane + fb]
            out[pl.ds(row, sub), pl.ds(lanes(1 - h), fb)] = far[m, at_row : at_row + sub, at_lane : at_lane + fb]


def join_body(own, far, tok, cot):
    tb = own.shape[1]
    half = tb // 2
    for m, full in enumerate((tok, cot)):
        for oc in range(2):
            full[oc * tb : oc * tb + half, :] = own[m, oc * half : (oc + 1) * half, :]
            full[oc * tb + half : (oc + 1) * tb, :] = far[m, oc * half : (oc + 1) * half, :]


def forward_body(tok, cot, *refs):
    columns, (gu, dn, keep, away) = refs[:4], refs[4:]
    tb = keep.shape[0]
    fb = columns[0].shape[-1]
    for f in range(2):
        for j in range(NX):
            column = columns[j]
            at = (f * NX + j) * fb
            for g in range(2):
                for e in range(2):
                    unit = (g * 2 + e) * fb
                    gu[at : at + fb, unit : unit + fb] = column[f * 2 + g, e, 0]
                    gu[at : at + fb, 4 * fb + unit : 4 * fb + unit + fb] = column[f * 2 + g, e, 1]
                    dn[unit : unit + fb, at : at + fb] = column[f * 2 + g, e, 2]
    wide = gu.shape[1]
    away[:, :wide] = nn(tok[tb:, :], gu[...]).astype(BF)
    away[:, wide:] = nt(cot[tb:, :], dn[...]).astype(BF)
    keep[:, :wide] = nn(tok[:tb, :], gu[...])
    keep[:, wide:] = nt(cot[:tb, :], dn[...])


def grad_body(f, da, dc, tok, cot, p1, p3, p2, p0):
    tb = da.shape[0]
    fb = p0.shape[-1]
    hid = 4 * fb
    for j, piece in ((1, p1), (3, p3), (2, p2), (0, p0)):
        at = (f * NX + j) * fb
        gu = tn(tok[:tb, at : at + fb], da[:, : 2 * hid]) + tn(tok[tb:, at : at + fb], dc[:, : 2 * hid])
        dn = tn(da[:, 2 * hid :], cot[:tb, at : at + fb]) + tn(dc[:, 2 * hid :], cot[tb:, at : at + fb])
        for g in range(2):
            for e in range(2):
                unit = (g * 2 + e) * fb
                piece[g, e, 0] = gu[:, unit : unit + fb].astype(piece.dtype)
                piece[g, e, 1] = gu[:, hid + unit : hid + unit + fb].astype(piece.dtype)
                piece[g, e, 2] = dn[unit : unit + fb].astype(piece.dtype)


def output_body(da, dc, gu, dn, own, oth):
    tb, wide = da.shape[0], gu.shape[1]
    half = tb // 2
    for oc, part in ((0, da), (1, dc)):
        out = nn(part[:, wide:], dn[...]).astype(BF)
        grad = nt(part[:, :wide], gu[...]).astype(BF)
        for m, rows in ((0, out), (1, grad)):
            own[m, oc * half : (oc + 1) * half, :] = rows[:half]
            oth[m, oc * half : (oc + 1) * half, :] = rows[half:]


def shards(tokens, gate_weight, up_weight, down_weight, cotangent):
    dp, t = lax.axis_index("dp"), lax.axis_index("tensor")
    z, h, x = dp // (NH * NX), (dp // NX) % NH, dp % NX
    where = jnp.stack([t, h, x, z // 4]).astype(jnp.int32)
    fb = gate_weight.shape[0]
    tb = tokens.shape[0]
    sub = tb // 4
    quarter = cotangent.shape[1]
    wide, hid = 8 * fb, 4 * fb

    with jax.named_scope("weights_core"):
        block = jnp.stack([gate_weight, up_weight, down_weight])
        pair = jnp.stack([block, send(block, swap_core)])

    with jax.named_scope("weights_turn"):
        column = jnp.stack([send(pair, turn(f, g)) for f in range(2) for g in range(2)])
    where, tokens, cotangent, _ = lax.optimization_barrier((where, tokens, cotangent, pair))
    with jax.named_scope("weights_x"):
        columns = [column] + [send(column, along_x(-j)) for j in range(1, NX)]
    with jax.named_scope("pick"):
        picked = lax.dynamic_slice(tokens, (0, t * quarter), (tb, quarter))
        own, oth = call(pick_body, [((2, tb, wide), BF)] * 2, [picked, cotangent], 0, where)
    with jax.named_scope("input_swap"):
        swapped = send(after(oth, column), swap_hi)
    with jax.named_scope("join"):
        tok, cot = call(join_body, [((2 * tb, wide), BF)] * 2, [own, swapped])

    product = 2 * 2 * tb * wide * hid
    with jax.named_scope("forward"):
        gu, dn, keep, away = call(
            forward_body,
            [((wide, 2 * hid), BF), ((hid, wide), BF), ((tb, 3 * hid), F32), ((tb, 3 * hid), BF)],
            [tok, cot, *columns],
            3 * product,
        )
    part = keep + send(away, swap_core).astype(F32)
    pre = part[:sub]
    for k in range(1, 4):
        pre = pre + send(part[k * sub : (k + 1) * sub].astype(BF), along_y(k)).astype(F32)
    gate_pre, up_pre, d_hidden = pre[:, :hid], pre[:, hid : 2 * hid], pre[:, 2 * hid :]
    sig = jax.nn.sigmoid(gate_pre)
    act = gate_pre * sig
    hidden = (act * up_pre).astype(BF)
    d_gate = (d_hidden * up_pre * sig * (1.0 + gate_pre * (1.0 - sig))).astype(BF)
    d_up = (d_hidden * act).astype(BF)
    mine = jnp.concatenate([d_gate, d_up, hidden], axis=1)
    four = jnp.concatenate([mine] + [send(mine, along_y(k)) for k in range(1, 4)], axis=0)
    terms = (four, send(four, swap_core))

    shape = (2, 2, 3, fb, fb)

    def pieces_of(f):
        return call(functools.partial(grad_body, f), [(shape, BF)] * 3 + [(shape, F32)], [*terms, tok, cot], 3 * product // 2)

    def summed(moved, kept):
        total = kept
        for piece in moved:
            total = total + piece.astype(F32)
        return total.astype(BF)

    def returned(f, total):
        with jax.named_scope(f"grads_turn_{f}"):
            return [send_back(total[g], turn(f, g)) for g in range(2)]

    with jax.named_scope("grads"):
        p1, p3, p2, p0 = pieces_of(0)
        q1, q3, q2, q0 = pieces_of(1)
    with jax.named_scope("grads_x_0"):
        p1, p3, p2 = send(p1, along_x(1)), send(p3, along_x(3)), send(p2, along_x(2))
    with jax.named_scope("outputs"):
        own, oth = call(output_body, [((2, tb, wide), BF)] * 2, [*terms, gu, dn], 3 * product)
    with jax.named_scope("output_swap"):
        swapped = send(oth, swap_hi)
    with jax.named_scope("place"):
        layer_out, token_grad = call(place_body, [((tb, quarter), BF)] * 2, [own, swapped], 0, where)
    p1, p3, q1, q3, q2, oth = lax.optimization_barrier((p1, p3, q1, q3, q2, oth))
    with jax.named_scope("grads_x_1"):
        q1, q3, q2 = send(q1, along_x(1)), send(q3, along_x(3)), send(q2, along_x(2))
    back = returned(0, summed((p1, p3, p2), p0))
    back = back + returned(1, after(summed((q1, q3, q2), q0), swapped))
    total = sum(piece.astype(F32) for piece in back)
    kept, moved, layer_out, token_grad = lax.optimization_barrier((total[0], total[1], layer_out, token_grad))
    with jax.named_scope("grads_core"):
        total = kept + send(moved, swap_core)
    return layer_out, token_grad, total[0], total[1], total[2]


def solution(mesh):
    placed = (
        P("dp", None),
        P("dp", "tensor"),
        P("dp", "tensor"),
        P("tensor", "dp"),
        P("dp", "tensor"),
    )
    return jax.shard_map(
        shards,
        mesh=mesh,
        in_specs=placed,
        out_specs=(
            P("dp", "tensor"),
            P("dp", "tensor"),
            P("dp", "tensor"),
            P("dp", "tensor"),
            P("tensor", "dp"),
        ),
        check_vma=False,
    )
```

```python
import functools

import jax
import jax.numpy as jnp
from jax import lax
from jax.experimental import pallas as pl
from jax.experimental.pallas import tpu as pltpu
from jax.sharding import PartitionSpec as P

NZ, NH, NX, NL, NC = 8, 2, 4, 2, 2
AXES = ("dp", "tensor")
BF = jnp.bfloat16
F32 = jnp.float32
VMEM_BYTES = 16 * 1024 * 1024


def index_of(z, h, x, l, c):
    return (((z * NH + h) * NX + x) * NL + l) * NC + c


def pairs_of(move):
    pairs = []
    for z in range(NZ):
        for h in range(NH):
            for x in range(NX):
                for l in range(NL):
                    for c in range(NC):
                        pairs.append((index_of(z, h, x, l, c), index_of(*move(z, h, x, l, c))))
    return pairs


def send(value, move):
    return lax.ppermute(value, AXES, pairs_of(move))


def send_back(value, move):
    return lax.ppermute(value, AXES, [(b, a) for a, b in pairs_of(move)])


def swap_hi(z, h, x, l, c):
    return z, 1 - h, x, l, c


def swap_core(z, h, x, l, c):
    return z, h, x, l, 1 - c


def along_x(step):
    return lambda z, h, x, l, c: (z, h, (x + step) % NX, l, c)


def along_y(k):
    return lambda z, h, x, l, c: (z, h ^ (k // 2), x, l ^ (k % 2), c)


def turn(f, g):
    def move(z, h, x, l, c):
        return 4 * ((z % 2) ^ f) + 2 * (l ^ g) + c, h, x, z // 4, (z // 2) % 2

    return move


def after(value, *others):
    return lax.optimization_barrier((value, *others))[0]


def nn(a, b):
    return jnp.dot(a, b, preferred_element_type=F32)


def tn(a, b):
    return lax.dot_general(a, b, (((0,), (0,)), ((), ())), preferred_element_type=F32)


def nt(a, b):
    return lax.dot_general(a, b, (((1,), (1,)), ((), ())), preferred_element_type=F32)


def call(body, shapes, args, flops=0, where=None):
    moved = sum(a.size * a.dtype.itemsize for a in args)
    moved += sum(functools.reduce(lambda p, q: p * q, s, 1) * jnp.dtype(d).itemsize for s, d in shapes)
    scalars = [] if where is None else [where]
    return pl.pallas_call(
        body,
        out_shape=[jax.ShapeDtypeStruct(s, d) for s, d in shapes],
        in_specs=[pl.BlockSpec(memory_space=pltpu.SMEM)] * len(scalars) + [pl.BlockSpec(memory_space=pltpu.VMEM)] * len(args),
        out_specs=[pl.BlockSpec(memory_space=pltpu.VMEM)] * len(shapes),
        compiler_params=pltpu.CompilerParams(vmem_limit_bytes=VMEM_BYTES),
        cost_estimate=pl.CostEstimate(flops=flops, bytes_accessed=moved, transcendentals=0),
    )(*scalars, *args)


def blocks_of(where, fb, sub):
    t, x, b = where[0], where[2], where[3]
    for oc in range(2):
        for ol in range(2):
            rows = pl.multiple_of((t ^ (2 * ol + oc)) * sub, sub)
            for r in range(2):
                for j in range(NX):
                    s = lax.rem(x + j, NX)

                    def lanes(half, r=r, s=s):
                        return pl.multiple_of((((r ^ b) * NH + half) * NX + s) * fb, fb)

                    yield (oc * 2 + ol) * sub, (r * NX + j) * fb, rows, lanes


def pick_body(where, tok, cot, own, oth):
    sub = tok.shape[0] // 4
    fb = tok.shape[1] // 16
    h = where[1]
    for m, source in enumerate((tok, cot)):
        for to_row, to_lane, row, lanes in blocks_of(where, fb, sub):
            oth[m, to_row : to_row + sub, to_lane : to_lane + fb] = source[pl.ds(row, sub), pl.ds(lanes(1 - h), fb)]
            own[m, to_row : to_row + sub, to_lane : to_lane + fb] = source[pl.ds(row, sub), pl.ds(lanes(h), fb)]


def place_body(where, own, far, layer_out, token_grad):
    sub = own.shape[1] // 4
    fb = own.shape[2] // 8
    h = where[1]
    for m, out in enumerate((layer_out, token_grad)):
        for at_row, at_lane, row, lanes in blocks_of(where, fb, sub):
            out[pl.ds(row, sub), pl.ds(lanes(h), fb)] = own[m, at_row : at_row + sub, at_lane : at_lane + fb]
            out[pl.ds(row, sub), pl.ds(lanes(1 - h), fb)] = far[m, at_row : at_row + sub, at_lane : at_lane + fb]


def join_body(own, far, tok, cot):
    tb = own.shape[1]
    half = tb // 2
    for m, full in enumerate((tok, cot)):
        for oc in range(2):
            full[oc * tb : oc * tb + half, :] = own[m, oc * half : (oc + 1) * half, :]
            full[oc * tb + half : (oc + 1) * tb, :] = far[m, oc * half : (oc + 1) * half, :]


def forward_body(tok, cot, c0, c1, c2, c3, gu, dn, keep, away):
    fb = c0.shape[-1]
    tb = keep.shape[0]
    for f in range(2):
        for j, column in enumerate((c0, c1, c2, c3)):
            at = (f * NX + j) * fb
            for e in range(2):
                gu[at : at + fb, e * fb : e * fb + fb] = column[f, e, 0]
                gu[at : at + fb, (2 + e) * fb : (2 + e) * fb + fb] = column[f, e, 1]
                dn[e * fb : e * fb + fb, at : at + fb] = column[f, e, 2]
    wide = gu.shape[1]
    away[:, :wide] = nn(tok[tb:, :], gu[...]).astype(BF)
    away[:, wide:] = nt(cot[tb:, :], dn[...]).astype(BF)
    keep[:, :wide] = nn(tok[:tb, :], gu[...])
    keep[:, wide:] = nt(cot[:tb, :], dn[...])


def grad_body(da, dc, tok, cot, p1, p3, p2, p0):
    tb = da.shape[0]
    fb = p0.shape[-1]
    wide = 4 * fb
    for j, piece in ((1, p1), (3, p3), (2, p2), (0, p0)):
        for f in range(2):
            at = (f * NX + j) * fb
            gu = tn(tok[:tb, at : at + fb], da[:, :wide]) + tn(tok[tb:, at : at + fb], dc[:, :wide])
            dn = tn(da[:, wide:], cot[:tb, at : at + fb]) + tn(dc[:, wide:], cot[tb:, at : at + fb])
            for e in range(2):
                piece[f, e, 0] = gu[:, e * fb : e * fb + fb].astype(piece.dtype)
                piece[f, e, 1] = gu[:, (2 + e) * fb : (2 + e) * fb + fb].astype(piece.dtype)
                piece[f, e, 2] = dn[e * fb : e * fb + fb].astype(piece.dtype)


def output_body(da, dc, ea, ec, gu_d, dn_d, gu_e, dn_e, own, oth):
    wide = gu_d.shape[1]
    half = da.shape[0] // 2
    for oc, d, e in ((0, da, ea), (1, dc, ec)):
        out = (nn(d[:, wide:], dn_d[...]) + nn(e[:, wide:], dn_e[...])).astype(BF)
        grad = (nt(d[:, :wide], gu_d[...]) + nt(e[:, :wide], gu_e[...])).astype(BF)
        for m, rows in ((0, out), (1, grad)):
            own[m, oc * half : (oc + 1) * half, :] = rows[:half]
            oth[m, oc * half : (oc + 1) * half, :] = rows[half:]


def shards(tokens, gate_weight, up_weight, down_weight, cotangent):
    dp, t = lax.axis_index("dp"), lax.axis_index("tensor")
    z, h, x = dp // (NH * NX), (dp // NX) % NH, dp % NX
    where = jnp.stack([t, h, x, z // 4]).astype(jnp.int32)
    fb = gate_weight.shape[0]
    tb = tokens.shape[0]
    sub = tb // 4
    quarter = cotangent.shape[1]
    wide, unit = 8 * fb, 2 * fb

    with jax.named_scope("weights_core"):
        block = jnp.stack([gate_weight, up_weight, down_weight])
        pair = jnp.stack([block, send(block, swap_core)])

    def turned(g, value):
        with jax.named_scope(f"weights_turn_{g}"):
            return [send(value, turn(f, g)) for f in range(2)]

    def along(g, column):
        with jax.named_scope(f"weights_x_{g}"):
            return [column] + [send(column, along_x(-j)) for j in range(1, NX)]

    first = jnp.stack(turned(0, pair))
    where, tokens, cotangent, _ = lax.optimization_barrier((where, tokens, cotangent, pair))
    second = jnp.stack(turned(1, after(pair, first)))
    with jax.named_scope("pick"):
        picked = lax.dynamic_slice(tokens, (0, t * quarter), (tb, quarter))
        own, oth = call(pick_body, [((2, tb, wide), BF)] * 2, [picked, cotangent], 0, where)
    with jax.named_scope("input_swap"):
        swapped = send(after(oth, first), swap_hi)
    with jax.named_scope("join"):
        tok, cot = call(join_body, [((2 * tb, wide), BF)] * 2, [own, swapped])
    first = along(0, first)
    first[0] = after(first[0], second)
    second = along(1, after(second, *first[1:]))

    product = 2 * 2 * tb * wide * unit

    def forward(g, columns, rows):
        with jax.named_scope(f"forward_{g}"):
            return call(
                forward_body,
                [((wide, 2 * unit), BF), ((unit, wide), BF), ((tb, 3 * unit), F32), ((tb, 3 * unit), BF)],
                [rows, cot, *columns],
                3 * product,
            )

    def core_reduced(g, keep, away):
        with jax.named_scope(f"reduce_core_{g}"):
            return keep + send(away, swap_core).astype(F32)

    def ring_reduced(g, part, *others):
        with jax.named_scope(f"reduce_ring_{g}"):
            total = after(part[:sub], *others)
            for k in range(1, 4):
                total = total + send(part[k * sub : (k + 1) * sub].astype(BF), along_y(k)).astype(F32)
            return total

    def activations(pre):
        gate_pre, up_pre, d_hidden = pre[:, :unit], pre[:, unit : 2 * unit], pre[:, 2 * unit :]
        sig = jax.nn.sigmoid(gate_pre)
        act = gate_pre * sig
        hidden = (act * up_pre).astype(BF)
        d_gate = (d_hidden * up_pre * sig * (1.0 + gate_pre * (1.0 - sig))).astype(BF)
        d_up = (d_hidden * act).astype(BF)
        return jnp.concatenate([d_gate, d_up, hidden], axis=1)

    def gathered(g, mine, *others):
        with jax.named_scope(f"gather_ring_{g}"):
            four = jnp.concatenate([mine] + [send(mine, along_y(k)) for k in range(1, 4)], axis=0)
        with jax.named_scope(f"gather_core_{g}"):
            return four, send(after(four, *others), swap_core)

    shape = (2, 2, 3, fb, fb)

    def pieces_of(g, terms):
        with jax.named_scope(f"grads_{g}"):
            return call(grad_body, [(shape, BF)] * 3 + [(shape, F32)], [*terms, tok, cot], 3 * product)

    def summed(moved, kept):
        total = kept
        for piece in moved:
            total = total + piece.astype(F32)
        return total.astype(BF)

    def returned(g, total):
        with jax.named_scope(f"grads_turn_{g}"):
            return [send_back(total[f], turn(f, g)) for f in range(2)]

    gu_0, dn_0, keep_0, away_0 = forward(0, first, tok)
    part_0 = core_reduced(0, keep_0, away_0)
    gu_1, dn_1, keep_1, away_1 = forward(1, second, after(tok, part_0))
    mine_0 = activations(ring_reduced(0, part_0, keep_1))
    mine_1 = activations(ring_reduced(1, core_reduced(1, keep_1, away_1)))
    terms_0 = gathered(0, mine_0, mine_1)
    p1, p3, p2, p0 = pieces_of(0, terms_0)
    with jax.named_scope("grads_x_0"):
        p1, p3, p2 = send(p1, along_x(1)), send(p3, along_x(3)), send(p2, along_x(2))

    terms_1 = gathered(1, mine_1, p1, p3, p2)
    q1, q3, q2, q0 = pieces_of(1, terms_1)
    with jax.named_scope("outputs"):
        own, oth = call(output_body, [((2, tb, wide), BF)] * 2, [*terms_0, *terms_1, after(gu_0, q0), dn_0, gu_1, dn_1], 6 * product)
    with jax.named_scope("output_swap"):
        swapped = send(oth, swap_hi)
    with jax.named_scope("place"):
        layer_out, token_grad = call(place_body, [((tb, quarter), BF)] * 2, [own, swapped], 0, where)
    back = returned(0, summed((p1, p3, p2), p0))
    with jax.named_scope("grads_x_1"):
        q1, q3, q2 = send(q1, along_x(1)), send(q3, along_x(3)), send(q2, along_x(2))
    back = back + returned(1, after(summed((q1, q3, q2), q0), swapped))
    total = sum(piece.astype(F32) for piece in back)
    kept, moved, layer_out, token_grad = lax.optimization_barrier((total[0], total[1], layer_out, token_grad))
    with jax.named_scope("grads_core"):
        total = kept + send(moved, swap_core)
    return layer_out, token_grad, total[0], total[1], total[2]


def solution(mesh):
    placed = (
        P("dp", None),
        P("dp", "tensor"),
        P("dp", "tensor"),
        P("tensor", "dp"),
        P("dp", "tensor"),
    )
    return jax.shard_map(
        shards,
        mesh=mesh,
        in_specs=placed,
        out_specs=(
            P("dp", "tensor"),
            P("dp", "tensor"),
            P("dp", "tensor"),
            P("dp", "tensor"),
            P("tensor", "dp"),
        ),
        check_vma=False,
    )
```

```python
import functools

import jax
import jax.numpy as jnp
from jax import lax
from jax.experimental import pallas as pl
from jax.experimental.pallas import tpu as pltpu
from jax.sharding import PartitionSpec as P

NZ, NH, NX, NL, NC = 8, 2, 4, 2, 2
AXES = ("dp", "tensor")
BF = jnp.bfloat16
F32 = jnp.float32
VMEM_BYTES = 16 * 1024 * 1024


def index_of(z, h, x, l, c):
    return (((z * NH + h) * NX + x) * NL + l) * NC + c


def pairs_of(move):
    pairs = []
    for z in range(NZ):
        for h in range(NH):
            for x in range(NX):
                for l in range(NL):
                    for c in range(NC):
                        pairs.append((index_of(z, h, x, l, c), index_of(*move(z, h, x, l, c))))
    return pairs


def send(value, move):
    return lax.ppermute(value, AXES, pairs_of(move))


def send_back(value, move):
    return lax.ppermute(value, AXES, [(b, a) for a, b in pairs_of(move)])


def swap_hi(z, h, x, l, c):
    return z, 1 - h, x, l, c


def swap_core(z, h, x, l, c):
    return z, h, x, l, 1 - c


def along_x(step):
    return lambda z, h, x, l, c: (z, h, x ^ step, l, c)


def along_y(k):
    return lambda z, h, x, l, c: (z, h ^ (k // 2), x, l ^ (k % 2), c)


def turn(f, g):
    def move(z, h, x, l, c):
        return 4 * (l ^ g) + 2 * c + ((z % 2) ^ f), h, x, z // 4, (z // 2) % 2

    return move


def after(value, *others):
    return lax.optimization_barrier((value, *others))[0]


def nn(a, b):
    return jnp.dot(a, b, preferred_element_type=F32)


def tn(a, b):
    return lax.dot_general(a, b, (((0,), (0,)), ((), ())), preferred_element_type=F32)


def nt(a, b):
    return lax.dot_general(a, b, (((1,), (1,)), ((), ())), preferred_element_type=F32)


def call(body, shapes, args, flops=0, where=None):
    moved = sum(a.size * a.dtype.itemsize for a in args)
    moved += sum(functools.reduce(lambda p, q: p * q, s, 1) * jnp.dtype(d).itemsize for s, d in shapes)
    scalars = [] if where is None else [where]
    return pl.pallas_call(
        body,
        out_shape=[jax.ShapeDtypeStruct(s, d) for s, d in shapes],
        in_specs=[pl.BlockSpec(memory_space=pltpu.SMEM)] * len(scalars) + [pl.BlockSpec(memory_space=pltpu.VMEM)] * len(args),
        out_specs=[pl.BlockSpec(memory_space=pltpu.VMEM)] * len(shapes),
        compiler_params=pltpu.CompilerParams(vmem_limit_bytes=VMEM_BYTES),
        cost_estimate=pl.CostEstimate(flops=flops, bytes_accessed=moved, transcendentals=0),
    )(*scalars, *args)


def blocks_of(where, fb, sub):
    t, x, b = where[0], where[2], where[3]
    for oc in range(2):
        for ol in range(2):
            rows = pl.multiple_of((t ^ (2 * ol + oc)) * sub, sub)
            for r in range(2):
                for j in range(NX):
                    s = x ^ j

                    def lanes(half, r=r, s=s):
                        return pl.multiple_of((((r ^ b) * NH + half) * NX + s) * fb, fb)

                    yield (oc * 2 + ol) * sub, (r * NX + j) * fb, rows, lanes


def pick_body(where, tok, cot, own, oth):
    sub = tok.shape[0] // 4
    fb = tok.shape[1] // 16
    h = where[1]
    for m, source in enumerate((tok, cot)):
        for to_row, to_lane, row, lanes in blocks_of(where, fb, sub):
            oth[m, to_row : to_row + sub, to_lane : to_lane + fb] = source[pl.ds(row, sub), pl.ds(lanes(1 - h), fb)]
            own[m, to_row : to_row + sub, to_lane : to_lane + fb] = source[pl.ds(row, sub), pl.ds(lanes(h), fb)]


def place_body(where, own, far, layer_out, token_grad):
    sub = own.shape[1] // 4
    fb = own.shape[2] // 8
    h = where[1]
    for m, out in enumerate((layer_out, token_grad)):
        for at_row, at_lane, row, lanes in blocks_of(where, fb, sub):
            out[pl.ds(row, sub), pl.ds(lanes(h), fb)] = own[m, at_row : at_row + sub, at_lane : at_lane + fb]
            out[pl.ds(row, sub), pl.ds(lanes(1 - h), fb)] = far[m, at_row : at_row + sub, at_lane : at_lane + fb]


def join_body(own, far, tok, cot):
    tb = own.shape[1]
    half = tb // 2
    for m, full in enumerate((tok, cot)):
        for oc in range(2):
            full[oc * tb : oc * tb + half, :] = own[m, oc * half : (oc + 1) * half, :]
            full[oc * tb + half : (oc + 1) * tb, :] = far[m, oc * half : (oc + 1) * half, :]


def forward_body(tok, cot, *refs):
    columns, (gu, dn, keep, away) = refs[:4], refs[4:]
    tb = keep.shape[0]
    fb = columns[0].shape[-1]
    for f in range(2):
        for j in range(NX):
            column = columns[j]
            at = (f * NX + j) * fb
            for g in range(2):
                for e in range(2):
                    unit = (g * 2 + e) * fb
                    gu[at : at + fb, unit : unit + fb] = column[f * 2 + g, e, 0]
                    gu[at : at + fb, 4 * fb + unit : 4 * fb + unit + fb] = column[f * 2 + g, e, 1]
                    dn[unit : unit + fb, at : at + fb] = column[f * 2 + g, e, 2]
    wide = gu.shape[1]
    away[:, :wide] = nn(tok[tb:, :], gu[...]).astype(BF)
    away[:, wide:] = nt(cot[tb:, :], dn[...]).astype(BF)
    keep[:, :wide] = nn(tok[:tb, :], gu[...])
    keep[:, wide:] = nt(cot[:tb, :], dn[...])


def grad_body(f, da, dc, tok, cot, p1, p3, p2, p0):
    tb = da.shape[0]
    fb = p0.shape[-1]
    hid = 4 * fb
    for j, piece in ((1, p1), (3, p3), (2, p2), (0, p0)):
        at = (f * NX + j) * fb
        gu = tn(tok[:tb, at : at + fb], da[:, : 2 * hid]) + tn(tok[tb:, at : at + fb], dc[:, : 2 * hid])
        dn = tn(da[:, 2 * hid :], cot[:tb, at : at + fb]) + tn(dc[:, 2 * hid :], cot[tb:, at : at + fb])
        for g in range(2):
            for e in range(2):
                unit = (g * 2 + e) * fb
                piece[g, e, 0] = gu[:, unit : unit + fb].astype(piece.dtype)
                piece[g, e, 1] = gu[:, hid + unit : hid + unit + fb].astype(piece.dtype)
                piece[g, e, 2] = dn[unit : unit + fb].astype(piece.dtype)


def output_body(da, dc, gu, dn, own, oth):
    tb, wide = da.shape[0], gu.shape[1]
    half = tb // 2
    for oc, part in ((0, da), (1, dc)):
        out = nn(part[:, wide:], dn[...]).astype(BF)
        grad = nt(part[:, :wide], gu[...]).astype(BF)
        for m, rows in ((0, out), (1, grad)):
            own[m, oc * half : (oc + 1) * half, :] = rows[:half]
            oth[m, oc * half : (oc + 1) * half, :] = rows[half:]


def shards(tokens, gate_weight, up_weight, down_weight, cotangent):
    dp, t = lax.axis_index("dp"), lax.axis_index("tensor")
    z, h, x = dp // (NH * NX), (dp // NX) % NH, dp % NX
    where = jnp.stack([t, h, x, z % 2]).astype(jnp.int32)
    fb = gate_weight.shape[0]
    tb = tokens.shape[0]
    sub = tb // 4
    quarter = cotangent.shape[1]
    wide, hid = 8 * fb, 4 * fb

    with jax.named_scope("weights_core"):
        block = jnp.stack([gate_weight, up_weight, down_weight])
        pair = jnp.stack([block, send(block, swap_core)])

    with jax.named_scope("weights_turn"):
        turned = [send(pair, turn(f, g)) for f in range(2) for g in range(2)]
        column = jnp.stack(turned)
    where, tokens, cotangent, _ = lax.optimization_barrier((where, tokens, cotangent, pair))
    with jax.named_scope("weights_x"):
        columns = [column] + [send(column, along_x(j)) for j in range(1, NX)]
    with jax.named_scope("pick"):
        picked = lax.dynamic_slice(tokens, (0, t * quarter), (tb, quarter))
        own, oth = call(pick_body, [((2, tb, wide), BF)] * 2, [picked, cotangent], 0, where)
    with jax.named_scope("input_swap"):
        swapped = send(after(oth, turned[0], turned[2]), swap_hi)
    with jax.named_scope("join"):
        tok, cot = call(join_body, [((2 * tb, wide), BF)] * 2, [own, swapped])

    product = 2 * 2 * tb * wide * hid
    with jax.named_scope("forward"):
        gu, dn, keep, away = call(
            forward_body,
            [((wide, 2 * hid), BF), ((hid, wide), BF), ((tb, 3 * hid), F32), ((tb, 3 * hid), BF)],
            [tok, cot, *columns],
            3 * product,
        )
    part = keep + send(away, swap_core).astype(F32)
    pre = part[:sub]
    for k in range(1, 4):
        pre = pre + send(part[k * sub : (k + 1) * sub].astype(BF), along_y(k)).astype(F32)
    gate_pre, up_pre, d_hidden = pre[:, :hid], pre[:, hid : 2 * hid], pre[:, 2 * hid :]
    sig = jax.nn.sigmoid(gate_pre)
    act = gate_pre * sig
    hidden = (act * up_pre).astype(BF)
    d_gate = (d_hidden * up_pre * sig * (1.0 + gate_pre * (1.0 - sig))).astype(BF)
    d_up = (d_hidden * act).astype(BF)
    mine = jnp.concatenate([d_gate, d_up, hidden], axis=1)
    four = jnp.concatenate([mine] + [send(mine, along_y(k)) for k in range(1, 4)], axis=0)
    terms = (four, send(four, swap_core))

    shape = (2, 2, 3, fb, fb)

    def pieces_of(f):
        return call(functools.partial(grad_body, f), [(shape, BF)] * 3 + [(shape, F32)], [*terms, tok, cot], 3 * product // 2)

    def summed(moved, kept):
        total = kept
        for piece in moved:
            total = total + piece.astype(F32)
        return total.astype(BF)

    def returned(f, total):
        with jax.named_scope(f"grads_turn_{f}"):
            return [send_back(total[g], turn(f, g)) for g in range(2)]

    with jax.named_scope("grads"):
        p1, p3, p2, p0 = pieces_of(0)
        q1, q3, q2, q0 = pieces_of(1)
    with jax.named_scope("grads_x_0"):
        p1, p3, p2 = send(p1, along_x(1)), send(p3, along_x(3)), send(p2, along_x(2))
    with jax.named_scope("outputs"):
        own, oth = call(output_body, [((2, tb, wide), BF)] * 2, [*terms, gu, dn], 3 * product)
    with jax.named_scope("output_swap"):
        swapped = send(oth, swap_hi)
    with jax.named_scope("place"):
        layer_out, token_grad = call(place_body, [((tb, quarter), BF)] * 2, [own, swapped], 0, where)
    with jax.named_scope("grads_x_1"):
        q1, q3, q2 = send(q1, along_x(1)), send(q3, along_x(3)), send(q2, along_x(2))
    back = returned(0, summed((p1, p3, p2), p0))
    back = back + returned(1, after(summed((q1, q3, q2), q0), swapped))
    total = sum(piece.astype(F32) for piece in back)
    kept, moved, layer_out, token_grad = lax.optimization_barrier((total[0], total[1], layer_out, token_grad))
    with jax.named_scope("grads_core"):
        total = kept + send(moved, swap_core)
    return layer_out, token_grad, total[0], total[1], total[2]


def solution(mesh):
    placed = (
        P("dp", None),
        P("dp", "tensor"),
        P("dp", "tensor"),
        P("tensor", "dp"),
        P("dp", "tensor"),
    )
    return jax.shard_map(
        shards,
        mesh=mesh,
        in_specs=placed,
        out_specs=(
            P("dp", "tensor"),
            P("dp", "tensor"),
            P("dp", "tensor"),
            P("dp", "tensor"),
            P("tensor", "dp"),
        ),
        check_vma=False,
    )
```

```python
import functools

import jax
import jax.numpy as jnp
from jax import lax
from jax.experimental import pallas as pl
from jax.experimental.pallas import tpu as pltpu
from jax.sharding import PartitionSpec as P

NZ, NH, NX, NL, NC = 8, 2, 4, 2, 2
AXES = ("dp", "tensor")
BF = jnp.bfloat16
F32 = jnp.float32
VMEM_BYTES = 16 * 1024 * 1024


def index_of(z, h, x, l, c):
    return (((z * NH + h) * NX + x) * NL + l) * NC + c


def pairs_of(move):
    pairs = []
    for z in range(NZ):
        for h in range(NH):
            for x in range(NX):
                for l in range(NL):
                    for c in range(NC):
                        pairs.append((index_of(z, h, x, l, c), index_of(*move(z, h, x, l, c))))
    return pairs


def send(value, move):
    return lax.ppermute(value, AXES, pairs_of(move))


def send_back(value, move):
    return lax.ppermute(value, AXES, [(b, a) for a, b in pairs_of(move)])


def swap_hi(z, h, x, l, c):
    return z, 1 - h, x, l, c


def swap_core(z, h, x, l, c):
    return z, h, x, l, 1 - c


def swap_plane(z, h, x, l, c):
    return z ^ 1, h, x, l, c


def along_x(step):
    return lambda z, h, x, l, c: (z, h, x ^ step, l, c)


def along_y(k):
    return lambda z, h, x, l, c: (z, h ^ (k // 2), x, l ^ (k % 2), c)


def turn(g):
    def move(z, h, x, l, c):
        return 4 * (l ^ g) + 2 * c + z % 2, h, x, z // 4, (z // 2) % 2

    return move


def after(value, *others):
    return lax.optimization_barrier((value, *others))[0]


def nn(a, b):
    return jnp.dot(a, b, preferred_element_type=F32)


def tn(a, b):
    return lax.dot_general(a, b, (((0,), (0,)), ((), ())), preferred_element_type=F32)


def nt(a, b):
    return lax.dot_general(a, b, (((1,), (1,)), ((), ())), preferred_element_type=F32)


def call(body, shapes, args, flops=0, where=None):
    moved = sum(a.size * a.dtype.itemsize for a in args)
    moved += sum(functools.reduce(lambda p, q: p * q, s, 1) * jnp.dtype(d).itemsize for s, d in shapes)
    scalars = [] if where is None else [where]
    return pl.pallas_call(
        body,
        out_shape=[jax.ShapeDtypeStruct(s, d) for s, d in shapes],
        in_specs=[pl.BlockSpec(memory_space=pltpu.SMEM)] * len(scalars) + [pl.BlockSpec(memory_space=pltpu.VMEM)] * len(args),
        out_specs=[pl.BlockSpec(memory_space=pltpu.VMEM)] * len(shapes),
        compiler_params=pltpu.CompilerParams(vmem_limit_bytes=VMEM_BYTES),
        cost_estimate=pl.CostEstimate(flops=flops, bytes_accessed=moved, transcendentals=0),
    )(*scalars, *args)


def blocks_of(where, fb, sub):
    t, x, b = where[0], where[2], where[3]
    for oc in range(2):
        for ol in range(2):
            rows = pl.multiple_of((t ^ (2 * ol + oc)) * sub, sub)
            for r in range(2):
                for j in range(NX):
                    s = x ^ j

                    def lanes(half, r=r, s=s):
                        return pl.multiple_of((((r ^ b) * NH + half) * NX + s) * fb, fb)

                    yield (oc * 2 + ol) * sub, (r * NX + j) * fb, rows, lanes


def pick_body(where, tok, cot, own, oth):
    sub = tok.shape[0] // 4
    fb = tok.shape[1] // 16
    h = where[1]
    for m, source in enumerate((tok, cot)):
        for to_row, to_lane, row, lanes in blocks_of(where, fb, sub):
            oth[m, to_row : to_row + sub, to_lane : to_lane + fb] = source[pl.ds(row, sub), pl.ds(lanes(1 - h), fb)]
            own[m, to_row : to_row + sub, to_lane : to_lane + fb] = source[pl.ds(row, sub), pl.ds(lanes(h), fb)]


def place_body(where, own, far, layer_out, token_grad):
    sub = own.shape[1] // 4
    fb = own.shape[2] // 8
    h = where[1]
    for m, out in enumerate((layer_out, token_grad)):
        for at_row, at_lane, row, lanes in blocks_of(where, fb, sub):
            out[pl.ds(row, sub), pl.ds(lanes(h), fb)] = own[m, at_row : at_row + sub, at_lane : at_lane + fb]
            out[pl.ds(row, sub), pl.ds(lanes(1 - h), fb)] = far[m, at_row : at_row + sub, at_lane : at_lane + fb]


def join_body(own, far, tok, cot):
    tb = own.shape[1]
    half = tb // 2
    for m, full in enumerate((tok, cot)):
        for oc in range(2):
            full[oc * tb : oc * tb + half, :] = own[m, oc * half : (oc + 1) * half, :]
            full[oc * tb + half : (oc + 1) * tb, :] = far[m, oc * half : (oc + 1) * half, :]


def forward_body(tok, cot, *refs):
    columns, (gu, dn, keep, away) = refs[:8], refs[8:]
    tb = keep.shape[0]
    fb = columns[0].shape[-1]
    for f in range(2):
        for j in range(NX):
            column = columns[f * NX + j]
            at = (f * NX + j) * fb
            for g in range(2):
                for e in range(2):
                    unit = (g * 2 + e) * fb
                    gu[at : at + fb, unit : unit + fb] = column[g, e, 0]
                    gu[at : at + fb, 4 * fb + unit : 4 * fb + unit + fb] = column[g, e, 1]
                    dn[unit : unit + fb, at : at + fb] = column[g, e, 2]
    wide = gu.shape[1]
    away[:, :wide] = nn(tok[tb:, :], gu[...]).astype(BF)
    away[:, wide:] = nt(cot[tb:, :], dn[...]).astype(BF)
    keep[:, :wide] = nn(tok[:tb, :], gu[...])
    keep[:, wide:] = nt(cot[:tb, :], dn[...])


def grad_body(f, da, dc, tok, cot, p1, p3, p2, p0):
    tb = da.shape[0]
    fb = p0.shape[-1]
    hid = 4 * fb
    for j, piece in ((1, p1), (3, p3), (2, p2), (0, p0)):
        at = (f * NX + j) * fb
        gu = tn(tok[:tb, at : at + fb], da[:, : 2 * hid]) + tn(tok[tb:, at : at + fb], dc[:, : 2 * hid])
        dn = tn(da[:, 2 * hid :], cot[:tb, at : at + fb]) + tn(dc[:, 2 * hid :], cot[tb:, at : at + fb])
        for g in range(2):
            for e in range(2):
                unit = (g * 2 + e) * fb
                piece[g, e, 0] = gu[:, unit : unit + fb].astype(piece.dtype)
                piece[g, e, 1] = gu[:, hid + unit : hid + unit + fb].astype(piece.dtype)
                piece[g, e, 2] = dn[unit : unit + fb].astype(piece.dtype)


def output_body(da, dc, gu, dn, own, oth):
    tb, wide = da.shape[0], gu.shape[1]
    half = tb // 2
    for oc, part in ((0, da), (1, dc)):
        out = nn(part[:, wide:], dn[...]).astype(BF)
        grad = nt(part[:, :wide], gu[...]).astype(BF)
        for m, rows in ((0, out), (1, grad)):
            own[m, oc * half : (oc + 1) * half, :] = rows[:half]
            oth[m, oc * half : (oc + 1) * half, :] = rows[half:]


def shards(tokens, gate_weight, up_weight, down_weight, cotangent):
    dp, t = lax.axis_index("dp"), lax.axis_index("tensor")
    z, h, x = dp // (NH * NX), (dp // NX) % NH, dp % NX
    where = jnp.stack([t, h, x, z % 2]).astype(jnp.int32)
    fb = gate_weight.shape[0]
    tb = tokens.shape[0]
    sub = tb // 4
    quarter = cotangent.shape[1]
    wide, hid = 8 * fb, 4 * fb

    with jax.named_scope("weights_core"):
        block = jnp.stack([gate_weight, up_weight, down_weight])
        pair = jnp.stack([block, send(block, swap_core)])

    with jax.named_scope("weights_turn"):
        near = jnp.stack([send(pair, turn(g)) for g in range(2)])
    with jax.named_scope("weights_plane"):
        far = send(near, swap_plane)
    where, tokens, cotangent, _ = lax.optimization_barrier((where, tokens, cotangent, pair))
    with jax.named_scope("pick"):
        picked = lax.dynamic_slice(tokens, (0, t * quarter), (tb, quarter))
        own, oth = call(pick_body, [((2, tb, wide), BF)] * 2, [picked, cotangent], 0, where)
    with jax.named_scope("input_swap"):
        swapped = send(after(oth, near), swap_hi)

    def along(f, column):
        with jax.named_scope(f"weights_x_{f}"):
            return [column] + [send(column, along_x(j)) for j in range(1, NX)]

    near = along(0, near)
    far = along(1, after(far, near[1], near[3]))
    with jax.named_scope("join"):
        tok, cot = call(join_body, [((2 * tb, wide), BF)] * 2, [own, swapped])

    product = 2 * 2 * tb * wide * hid
    with jax.named_scope("forward"):
        gu, dn, keep, away = call(
            forward_body,
            [((wide, 2 * hid), BF), ((hid, wide), BF), ((tb, 3 * hid), F32), ((tb, 3 * hid), BF)],
            [tok, cot, *near, *far],
            3 * product,
        )
    part = keep + send(away, swap_core).astype(F32)
    pre = part[:sub]
    for k in range(1, 4):
        pre = pre + send(part[k * sub : (k + 1) * sub].astype(BF), along_y(k)).astype(F32)
    gate_pre, up_pre, d_hidden = pre[:, :hid], pre[:, hid : 2 * hid], pre[:, 2 * hid :]
    sig = jax.nn.sigmoid(gate_pre)
    act = gate_pre * sig
    hidden = (act * up_pre).astype(BF)
    d_gate = (d_hidden * up_pre * sig * (1.0 + gate_pre * (1.0 - sig))).astype(BF)
    d_up = (d_hidden * act).astype(BF)
    mine = jnp.concatenate([d_gate, d_up, hidden], axis=1)
    four = jnp.concatenate([mine] + [send(mine, along_y(k)) for k in range(1, 4)], axis=0)
    terms = (four, send(four, swap_core))

    shape = (2, 2, 3, fb, fb)

    def pieces_of(f):
        return call(functools.partial(grad_body, f), [(shape, BF)] * 3 + [(shape, F32)], [*terms, tok, cot], 3 * product // 2)

    def summed(moved, kept):
        total = kept
        for piece in moved:
            total = total + piece.astype(F32)
        return total.astype(BF)

    with jax.named_scope("grads"):
        q1, q3, q2, q0 = pieces_of(1)
        p1, p3, p2, p0 = pieces_of(0)
    with jax.named_scope("grads_x_1"):
        q1, q3, q2 = send(q1, along_x(1)), send(q3, along_x(3)), send(q2, along_x(2))
    with jax.named_scope("outputs"):
        own, oth = call(output_body, [((2, tb, wide), BF)] * 2, [*terms, gu, dn], 3 * product)
    with jax.named_scope("output_swap"):
        swapped = send(oth, swap_hi)
    with jax.named_scope("place"):
        layer_out, token_grad = call(place_body, [((tb, quarter), BF)] * 2, [own, swapped], 0, where)
    with jax.named_scope("grads_x_0"):
        p1, p3, p2 = send(p1, along_x(1)), send(p3, along_x(3)), send(p2, along_x(2))
    with jax.named_scope("grads_plane"):
        q0 = send(summed((q1, q3, q2), q0), swap_plane)
    total = after(summed((p1, p3, p2, q0), p0), swapped)
    with jax.named_scope("grads_turn"):
        total = sum(send_back(total[g], turn(g)).astype(F32) for g in range(2))
    kept, moved, layer_out, token_grad = lax.optimization_barrier((total[0], total[1], layer_out, token_grad))
    with jax.named_scope("grads_core"):
        total = kept + send(moved, swap_core)
    return layer_out, token_grad, total[0], total[1], total[2]


def solution(mesh):
    placed = (
        P("dp", None),
        P("dp", "tensor"),
        P("dp", "tensor"),
        P("tensor", "dp"),
        P("dp", "tensor"),
    )
    return jax.shard_map(
        shards,
        mesh=mesh,
        in_specs=placed,
        out_specs=(
            P("dp", "tensor"),
            P("dp", "tensor"),
            P("dp", "tensor"),
            P("dp", "tensor"),
            P("tensor", "dp"),
        ),
        check_vma=False,
    )
```

```python
import functools

import jax
import jax.numpy as jnp
from jax import lax
from jax.experimental import pallas as pl
from jax.experimental.pallas import tpu as pltpu
from jax.sharding import PartitionSpec as P

NZ, NH, NX, NL, NC = 8, 2, 4, 2, 2
AXES = ("dp", "tensor")
BF = jnp.bfloat16
F32 = jnp.float32
VMEM_BYTES = 16 * 1024 * 1024


def index_of(z, h, x, l, c):
    return (((z * NH + h) * NX + x) * NL + l) * NC + c


def pairs_of(move):
    pairs = []
    for z in range(NZ):
        for h in range(NH):
            for x in range(NX):
                for l in range(NL):
                    for c in range(NC):
                        pairs.append((index_of(z, h, x, l, c), index_of(*move(z, h, x, l, c))))
    return pairs


def send(value, move):
    return lax.ppermute(value, AXES, pairs_of(move))


def send_back(value, move):
    return lax.ppermute(value, AXES, [(b, a) for a, b in pairs_of(move)])


def swap_hi(z, h, x, l, c):
    return z, 1 - h, x, l, c


def swap_core(z, h, x, l, c):
    return z, h, x, l, 1 - c


def swap_plane(z, h, x, l, c):
    return z ^ 1, h, x, l, c


def along_x(step):
    return lambda z, h, x, l, c: (z, h, x ^ step, l, c)


def along_y(k):
    return lambda z, h, x, l, c: (z, h ^ (k // 2), x, l ^ (k % 2), c)


def turn(g, e=0):
    def move(z, h, x, l, c):
        return 4 * (l ^ g) + 2 * (c ^ e) + z % 2, h, x, z // 4, (z // 2) % 2

    return move


def after(value, *others):
    return lax.optimization_barrier((value, *others))[0]


def nn(a, b):
    return jnp.dot(a, b, preferred_element_type=F32)


def tn(a, b):
    return lax.dot_general(a, b, (((0,), (0,)), ((), ())), preferred_element_type=F32)


def nt(a, b):
    return lax.dot_general(a, b, (((1,), (1,)), ((), ())), preferred_element_type=F32)


def call(body, shapes, args, flops=0, where=None):
    moved = sum(a.size * a.dtype.itemsize for a in args)
    moved += sum(functools.reduce(lambda p, q: p * q, s, 1) * jnp.dtype(d).itemsize for s, d in shapes)
    scalars = [] if where is None else [where]
    return pl.pallas_call(
        body,
        out_shape=[jax.ShapeDtypeStruct(s, d) for s, d in shapes],
        in_specs=[pl.BlockSpec(memory_space=pltpu.SMEM)] * len(scalars) + [pl.BlockSpec(memory_space=pltpu.VMEM)] * len(args),
        out_specs=[pl.BlockSpec(memory_space=pltpu.VMEM)] * len(shapes),
        compiler_params=pltpu.CompilerParams(vmem_limit_bytes=VMEM_BYTES),
        cost_estimate=pl.CostEstimate(flops=flops, bytes_accessed=moved, transcendentals=0),
    )(*scalars, *args)


def blocks_of(where, fb, sub):
    t, x, b = where[0], where[2], where[3]
    for oc in range(2):
        for ol in range(2):
            rows = pl.multiple_of((t ^ (2 * ol + oc)) * sub, sub)
            for r in range(2):
                for j in range(NX):
                    s = x ^ j

                    def lanes(half, r=r, s=s):
                        return pl.multiple_of((((r ^ b) * NH + half) * NX + s) * fb, fb)

                    yield (oc * 2 + ol) * sub, (r * NX + j) * fb, rows, lanes


def pick_body(where, tok, cot, own, oth):
    sub = tok.shape[0] // 4
    fb = tok.shape[1] // 16
    h = where[1]
    for m, source in enumerate((tok, cot)):
        for to_row, to_lane, row, lanes in blocks_of(where, fb, sub):
            oth[m, to_row : to_row + sub, to_lane : to_lane + fb] = source[pl.ds(row, sub), pl.ds(lanes(1 - h), fb)]
            own[m, to_row : to_row + sub, to_lane : to_lane + fb] = source[pl.ds(row, sub), pl.ds(lanes(h), fb)]


def place_body(where, own, far, layer_out, token_grad):
    sub = own.shape[1] // 4
    fb = own.shape[2] // 8
    h = where[1]
    for m, out in enumerate((layer_out, token_grad)):
        for at_row, at_lane, row, lanes in blocks_of(where, fb, sub):
            out[pl.ds(row, sub), pl.ds(lanes(h), fb)] = own[m, at_row : at_row + sub, at_lane : at_lane + fb]
            out[pl.ds(row, sub), pl.ds(lanes(1 - h), fb)] = far[m, at_row : at_row + sub, at_lane : at_lane + fb]


def join_body(own, far, tok, cot):
    tb = own.shape[1]
    half = tb // 2
    for m, full in enumerate((tok, cot)):
        for oc in range(2):
            full[oc * tb : oc * tb + half, :] = own[m, oc * half : (oc + 1) * half, :]
            full[oc * tb + half : (oc + 1) * tb, :] = far[m, oc * half : (oc + 1) * half, :]


def forward_body(tok, cot, *refs):
    columns, (gu, dn, keep, away) = refs[:8], refs[8:]
    tb = keep.shape[0]
    fb = columns[0].shape[-1]
    for f in range(2):
        for j in range(NX):
            column = columns[f * NX + j]
            at = (f * NX + j) * fb
            for g in range(2):
                for e in range(2):
                    unit = (g * 2 + e) * fb
                    gu[at : at + fb, unit : unit + fb] = column[g, e, 0]
                    gu[at : at + fb, 4 * fb + unit : 4 * fb + unit + fb] = column[g, e, 1]
                    dn[unit : unit + fb, at : at + fb] = column[g, e, 2]
    wide = gu.shape[1]
    away[:, :wide] = nn(tok[tb:, :], gu[...]).astype(BF)
    away[:, wide:] = nt(cot[tb:, :], dn[...]).astype(BF)
    keep[:, :wide] = nn(tok[:tb, :], gu[...])
    keep[:, wide:] = nt(cot[:tb, :], dn[...])


def grad_body(f, da, dc, tok, cot, p1, p3, p2, p0):
    tb = da.shape[0]
    fb = p0.shape[-1]
    hid = 4 * fb
    for j, piece in ((1, p1), (3, p3), (2, p2), (0, p0)):
        at = (f * NX + j) * fb
        gu = tn(tok[:tb, at : at + fb], da[:, : 2 * hid]) + tn(tok[tb:, at : at + fb], dc[:, : 2 * hid])
        dn = tn(da[:, 2 * hid :], cot[:tb, at : at + fb]) + tn(dc[:, 2 * hid :], cot[tb:, at : at + fb])
        for g in range(2):
            for e in range(2):
                unit = (g * 2 + e) * fb
                piece[g, e, 0] = gu[:, unit : unit + fb].astype(piece.dtype)
                piece[g, e, 1] = gu[:, hid + unit : hid + unit + fb].astype(piece.dtype)
                piece[g, e, 2] = dn[unit : unit + fb].astype(piece.dtype)


def output_body(da, dc, gu, dn, own, oth):
    tb, wide = da.shape[0], gu.shape[1]
    half = tb // 2
    for oc, part in ((0, da), (1, dc)):
        out = nn(part[:, wide:], dn[...]).astype(BF)
        grad = nt(part[:, :wide], gu[...]).astype(BF)
        for m, rows in ((0, out), (1, grad)):
            own[m, oc * half : (oc + 1) * half, :] = rows[:half]
            oth[m, oc * half : (oc + 1) * half, :] = rows[half:]


def shards(tokens, gate_weight, up_weight, down_weight, cotangent):
    dp, t = lax.axis_index("dp"), lax.axis_index("tensor")
    z, h, x = dp // (NH * NX), (dp // NX) % NH, dp % NX
    where = jnp.stack([t, h, x, z % 2]).astype(jnp.int32)
    fb = gate_weight.shape[0]
    tb = tokens.shape[0]
    sub = tb // 4
    quarter = cotangent.shape[1]
    wide, hid = 8 * fb, 4 * fb

    with jax.named_scope("weights_core"):
        block = jnp.stack([gate_weight, up_weight, down_weight])
        pair = jnp.stack([block, send(block, swap_core)])

    with jax.named_scope("weights_turn"):
        near = jnp.stack([send(pair, turn(g)) for g in range(2)])
    with jax.named_scope("weights_plane"):
        far = send(near, swap_plane)
    where, tokens, cotangent, _ = lax.optimization_barrier((where, tokens, cotangent, pair))
    with jax.named_scope("pick"):
        picked = lax.dynamic_slice(tokens, (0, t * quarter), (tb, quarter))
        own, oth = call(pick_body, [((2, tb, wide), BF)] * 2, [picked, cotangent], 0, where)
    with jax.named_scope("input_swap"):
        swapped = send(after(oth, near), swap_hi)

    def along(f, column):
        with jax.named_scope(f"weights_x_{f}"):
            return [column] + [send(column, along_x(j)) for j in range(1, NX)]

    near = along(0, near)
    far = along(1, after(far, near[1], near[3]))
    with jax.named_scope("join"):
        tok, cot = call(join_body, [((2 * tb, wide), BF)] * 2, [own, swapped])

    product = 2 * 2 * tb * wide * hid
    with jax.named_scope("forward"):
        gu, dn, keep, away = call(
            forward_body,
            [((wide, 2 * hid), BF), ((hid, wide), BF), ((tb, 3 * hid), F32), ((tb, 3 * hid), BF)],
            [tok, cot, *near, *far],
            3 * product,
        )
    part = keep + send(away, swap_core).astype(F32)
    pre = part[:sub]
    for k in range(1, 4):
        pre = pre + send(part[k * sub : (k + 1) * sub].astype(BF), along_y(k)).astype(F32)
    gate_pre, up_pre, d_hidden = pre[:, :hid], pre[:, hid : 2 * hid], pre[:, 2 * hid :]
    sig = jax.nn.sigmoid(gate_pre)
    act = gate_pre * sig
    hidden = (act * up_pre).astype(BF)
    d_gate = (d_hidden * up_pre * sig * (1.0 + gate_pre * (1.0 - sig))).astype(BF)
    d_up = (d_hidden * act).astype(BF)
    mine = jnp.concatenate([d_gate, d_up, hidden], axis=1)
    four = jnp.concatenate([mine] + [send(mine, along_y(k)) for k in range(1, 4)], axis=0)
    terms = (four, send(four, swap_core))

    shape = (2, 2, 3, fb, fb)

    def pieces_of(f):
        return call(functools.partial(grad_body, f), [(shape, BF)] * 3 + [(shape, F32)], [*terms, tok, cot], 3 * product // 2)

    def summed(moved, kept):
        total = kept
        for piece in moved:
            total = total + piece.astype(F32)
        return total.astype(BF)

    with jax.named_scope("grads"):
        q1, q3, q2, q0 = pieces_of(1)
        p1, p3, p2, p0 = pieces_of(0)
    with jax.named_scope("grads_x_1"):
        q1, q3, q2 = send(q1, along_x(1)), send(q3, along_x(3)), send(q2, along_x(2))
    with jax.named_scope("outputs"):
        own, oth = call(output_body, [((2, tb, wide), BF)] * 2, [*terms, gu, dn], 3 * product)
    with jax.named_scope("output_swap"):
        swapped = send(oth, swap_hi)
    with jax.named_scope("place"):
        layer_out, token_grad = call(place_body, [((tb, quarter), BF)] * 2, [own, swapped], 0, where)
    with jax.named_scope("grads_x_0"):
        p1, p3, p2 = send(p1, along_x(1)), send(p3, along_x(3)), send(p2, along_x(2))
    with jax.named_scope("grads_plane"):
        q0 = send(summed((q1, q3, q2), q0), swap_plane)
    total = after(summed((p1, p3, p2, q0), p0), swapped)
    with jax.named_scope("grads_turn"):
        pieces = [send_back(total[g, e], turn(g, e)) for g in range(2) for e in range(2)]
    *pieces, layer_out, token_grad = lax.optimization_barrier((*pieces, layer_out, token_grad))
    total = sum(piece.astype(F32) for piece in pieces)
    return layer_out, token_grad, total[0], total[1], total[2]


def solution(mesh):
    placed = (
        P("dp", None),
        P("dp", "tensor"),
        P("dp", "tensor"),
        P("tensor", "dp"),
        P("dp", "tensor"),
    )
    return jax.shard_map(
        shards,
        mesh=mesh,
        in_specs=placed,
        out_specs=(
            P("dp", "tensor"),
            P("dp", "tensor"),
            P("dp", "tensor"),
            P("dp", "tensor"),
            P("tensor", "dp"),
        ),
        check_vma=False,
    )
```

```python
import functools

import jax
import jax.numpy as jnp
from jax import lax
from jax.experimental import pallas as pl
from jax.experimental.pallas import tpu as pltpu
from jax.sharding import PartitionSpec as P

NZ, NH, NX, NL, NC = 8, 2, 4, 2, 2
AXES = ("dp", "tensor")
BF = jnp.bfloat16
F32 = jnp.float32
VMEM_BYTES = 16 * 1024 * 1024


def index_of(z, h, x, l, c):
    return (((z * NH + h) * NX + x) * NL + l) * NC + c


def pairs_of(move):
    pairs = []
    for z in range(NZ):
        for h in range(NH):
            for x in range(NX):
                for l in range(NL):
                    for c in range(NC):
                        pairs.append((index_of(z, h, x, l, c), index_of(*move(z, h, x, l, c))))
    return pairs


def send(value, move):
    return lax.ppermute(value, AXES, pairs_of(move))


def send_back(value, move):
    return lax.ppermute(value, AXES, [(b, a) for a, b in pairs_of(move)])


def swap_hi(z, h, x, l, c):
    return z, 1 - h, x, l, c


def swap_core(z, h, x, l, c):
    return z, h, x, l, 1 - c


def swap_plane(z, h, x, l, c):
    return z ^ 1, h, x, l, c


def along_x(step):
    return lambda z, h, x, l, c: (z, h, x ^ step, l, c)


def along_y(k):
    return lambda z, h, x, l, c: (z, h ^ (k // 2), x, l ^ (k % 2), c)


def turn(g, e=0):
    def move(z, h, x, l, c):
        return 4 * (l ^ g) + 2 * (c ^ e) + z % 2, h, x, z // 4, (z // 2) % 2

    return move


def after(value, *others):
    return lax.optimization_barrier((value, *others))[0]


def nn(a, b):
    return jnp.dot(a, b, preferred_element_type=F32)


def tn(a, b):
    return lax.dot_general(a, b, (((0,), (0,)), ((), ())), preferred_element_type=F32)


def nt(a, b):
    return lax.dot_general(a, b, (((1,), (1,)), ((), ())), preferred_element_type=F32)


def call(body, shapes, args, flops=0, where=None):
    moved = sum(a.size * a.dtype.itemsize for a in args)
    moved += sum(functools.reduce(lambda p, q: p * q, s, 1) * jnp.dtype(d).itemsize for s, d in shapes)
    scalars = [] if where is None else [where]
    return pl.pallas_call(
        body,
        out_shape=[jax.ShapeDtypeStruct(s, d) for s, d in shapes],
        in_specs=[pl.BlockSpec(memory_space=pltpu.SMEM)] * len(scalars) + [pl.BlockSpec(memory_space=pltpu.VMEM)] * len(args),
        out_specs=[pl.BlockSpec(memory_space=pltpu.VMEM)] * len(shapes),
        compiler_params=pltpu.CompilerParams(vmem_limit_bytes=VMEM_BYTES),
        cost_estimate=pl.CostEstimate(flops=flops, bytes_accessed=moved, transcendentals=0),
    )(*scalars, *args)


def blocks_of(where, fb, sub):
    t, x, b = where[0], where[2], where[3]
    for oc in range(2):
        for ol in range(2):
            rows = pl.multiple_of((t ^ (2 * ol + oc)) * sub, sub)
            for r in range(2):
                for j in range(NX):
                    s = x ^ j

                    def lanes(half, r=r, s=s):
                        return pl.multiple_of((((r ^ b) * NH + half) * NX + s) * fb, fb)

                    yield (oc * 2 + ol) * sub, (r * NX + j) * fb, rows, lanes


def pick_body(where, tok, cot, own, oth):
    sub = tok.shape[0] // 4
    fb = tok.shape[1] // 16
    h = where[1]
    for m, source in enumerate((tok, cot)):
        for to_row, to_lane, row, lanes in blocks_of(where, fb, sub):
            oth[m, to_row : to_row + sub, to_lane : to_lane + fb] = source[pl.ds(row, sub), pl.ds(lanes(1 - h), fb)]
            own[m, to_row : to_row + sub, to_lane : to_lane + fb] = source[pl.ds(row, sub), pl.ds(lanes(h), fb)]


def place_body(where, own, far, layer_out, token_grad):
    sub = own.shape[1] // 4
    fb = own.shape[2] // 8
    h = where[1]
    for m, out in enumerate((layer_out, token_grad)):
        for at_row, at_lane, row, lanes in blocks_of(where, fb, sub):
            out[pl.ds(row, sub), pl.ds(lanes(h), fb)] = own[m, at_row : at_row + sub, at_lane : at_lane + fb]
            out[pl.ds(row, sub), pl.ds(lanes(1 - h), fb)] = far[m, at_row : at_row + sub, at_lane : at_lane + fb]


def join_body(own, far, tok, cot):
    tb = own.shape[1]
    half = tb // 2
    for m, full in enumerate((tok, cot)):
        for oc in range(2):
            full[oc * tb : oc * tb + half, :] = own[m, oc * half : (oc + 1) * half, :]
            full[oc * tb + half : (oc + 1) * tb, :] = far[m, oc * half : (oc + 1) * half, :]


def forward_body(tok, cot, *refs):
    columns, (gu, dn, keep, away) = refs[:8], refs[8:]
    tb = keep.shape[0]
    fb = columns[0].shape[-1]
    for f in range(2):
        for j in range(NX):
            column = columns[f * NX + j]
            at = (f * NX + j) * fb
            for g in range(2):
                for e in range(2):
                    unit = (g * 2 + e) * fb
                    gu[at : at + fb, unit : unit + fb] = column[g, e, 0]
                    gu[at : at + fb, 4 * fb + unit : 4 * fb + unit + fb] = column[g, e, 1]
                    dn[unit : unit + fb, at : at + fb] = column[g, e, 2]
    wide = gu.shape[1]
    away[:, :wide] = nn(tok[tb:, :], gu[...]).astype(BF)
    away[:, wide:] = nt(cot[tb:, :], dn[...]).astype(BF)
    keep[:, :wide] = nn(tok[:tb, :], gu[...])
    keep[:, wide:] = nt(cot[:tb, :], dn[...])


def grad_body(f, da, dc, tok, cot, p1, p3, p2, p0):
    tb = da.shape[0]
    fb = p0.shape[-1]
    hid = 4 * fb
    for j, piece in ((1, p1), (3, p3), (2, p2), (0, p0)):
        at = (f * NX + j) * fb
        gu = tn(tok[:tb, at : at + fb], da[:, : 2 * hid]) + tn(tok[tb:, at : at + fb], dc[:, : 2 * hid])
        dn = tn(da[:, 2 * hid :], cot[:tb, at : at + fb]) + tn(dc[:, 2 * hid :], cot[tb:, at : at + fb])
        for g in range(2):
            for e in range(2):
                unit = (g * 2 + e) * fb
                piece[g, e, 0] = gu[:, unit : unit + fb].astype(piece.dtype)
                piece[g, e, 1] = gu[:, hid + unit : hid + unit + fb].astype(piece.dtype)
                piece[g, e, 2] = dn[unit : unit + fb].astype(piece.dtype)


def output_body(da, dc, gu, dn, own, oth):
    tb, wide = da.shape[0], gu.shape[1]
    half = tb // 2
    for oc, part in ((0, da), (1, dc)):
        out = nn(part[:, wide:], dn[...]).astype(BF)
        grad = nt(part[:, :wide], gu[...]).astype(BF)
        for m, rows in ((0, out), (1, grad)):
            own[m, oc * half : (oc + 1) * half, :] = rows[:half]
            oth[m, oc * half : (oc + 1) * half, :] = rows[half:]


def shards(tokens, gate_weight, up_weight, down_weight, cotangent):
    dp, t = lax.axis_index("dp"), lax.axis_index("tensor")
    z, h, x = dp // (NH * NX), (dp // NX) % NH, dp % NX
    where = jnp.stack([t, h, x, z % 2]).astype(jnp.int32)
    fb = gate_weight.shape[0]
    tb = tokens.shape[0]
    sub = tb // 4
    quarter = cotangent.shape[1]
    wide, hid = 8 * fb, 4 * fb

    with jax.named_scope("weights"):
        block = jnp.stack([gate_weight, up_weight, down_weight])
    with jax.named_scope("weights_turn"):
        turned = [send(block, turn(g, e)) for g in range(2) for e in range(2)]
        near = jnp.stack(turned).reshape(2, 2, *block.shape)
    with jax.named_scope("weights_plane"):
        far = send(near, swap_plane)
    where, tokens, cotangent, _ = lax.optimization_barrier((where, tokens, cotangent, block))
    with jax.named_scope("pick"):
        picked = lax.dynamic_slice(tokens, (0, t * quarter), (tb, quarter))
        own, oth = call(pick_body, [((2, tb, wide), BF)] * 2, [picked, cotangent], 0, where)
    with jax.named_scope("input_swap"):
        swapped = send(after(oth, near), swap_hi)

    def along(f, column):
        with jax.named_scope(f"weights_x_{f}"):
            return [column] + [send(column, along_x(j)) for j in range(1, NX)]

    near = along(0, near)
    far = along(1, after(far, near[1], near[3]))
    with jax.named_scope("join"):
        tok, cot = call(join_body, [((2 * tb, wide), BF)] * 2, [own, swapped])

    product = 2 * 2 * tb * wide * hid
    with jax.named_scope("forward"):
        gu, dn, keep, away = call(
            forward_body,
            [((wide, 2 * hid), BF), ((hid, wide), BF), ((tb, 3 * hid), F32), ((tb, 3 * hid), BF)],
            [tok, cot, *near, *far],
            3 * product,
        )
    part = keep + send(away, swap_core).astype(F32)
    pre = part[:sub]
    for k in range(1, 4):
        pre = pre + send(part[k * sub : (k + 1) * sub].astype(BF), along_y(k)).astype(F32)
    gate_pre, up_pre, d_hidden = pre[:, :hid], pre[:, hid : 2 * hid], pre[:, 2 * hid :]
    sig = jax.nn.sigmoid(gate_pre)
    act = gate_pre * sig
    hidden = (act * up_pre).astype(BF)
    d_gate = (d_hidden * up_pre * sig * (1.0 + gate_pre * (1.0 - sig))).astype(BF)
    d_up = (d_hidden * act).astype(BF)
    mine = jnp.concatenate([d_gate, d_up, hidden], axis=1)
    four = jnp.concatenate([mine] + [send(mine, along_y(k)) for k in range(1, 4)], axis=0)
    terms = (four, send(four, swap_core))

    shape = (2, 2, 3, fb, fb)

    def pieces_of(f):
        return call(functools.partial(grad_body, f), [(shape, BF)] * 3 + [(shape, F32)], [*terms, tok, cot], 3 * product // 2)

    def summed(moved, kept):
        total = kept
        for piece in moved:
            total = total + piece.astype(F32)
        return total.astype(BF)

    with jax.named_scope("grads"):
        q1, q3, q2, q0 = pieces_of(1)
        p1, p3, p2, p0 = pieces_of(0)
    with jax.named_scope("grads_x_1"):
        q1, q3, q2 = send(q1, along_x(1)), send(q3, along_x(3)), send(q2, along_x(2))
    with jax.named_scope("outputs"):
        own, oth = call(output_body, [((2, tb, wide), BF)] * 2, [*terms, gu, dn], 3 * product)
    with jax.named_scope("output_swap"):
        swapped = send(oth, swap_hi)
    with jax.named_scope("place"):
        layer_out, token_grad = call(place_body, [((tb, quarter), BF)] * 2, [own, swapped], 0, where)
    with jax.named_scope("grads_x_0"):
        p1, p3, p2 = send(p1, along_x(1)), send(p3, along_x(3)), send(p2, along_x(2))
    with jax.named_scope("grads_plane"):
        q0 = send(summed((q1, q3, q2), q0), swap_plane)
    total = after(summed((p1, p3, p2, q0), p0), swapped)
    with jax.named_scope("grads_turn"):
        pieces = [send_back(total[g, e], turn(g, e)) for g in range(2) for e in range(2)]
    *pieces, layer_out, token_grad = lax.optimization_barrier((*pieces, layer_out, token_grad))
    total = sum(piece.astype(F32) for piece in pieces)
    return layer_out, token_grad, total[0], total[1], total[2]


def solution(mesh):
    placed = (
        P("dp", None),
        P("dp", "tensor"),
        P("dp", "tensor"),
        P("tensor", "dp"),
        P("dp", "tensor"),
    )
    return jax.shard_map(
        shards,
        mesh=mesh,
        in_specs=placed,
        out_specs=(
            P("dp", "tensor"),
            P("dp", "tensor"),
            P("dp", "tensor"),
            P("dp", "tensor"),
            P("tensor", "dp"),
        ),
        check_vma=False,
    )
```

```python
import functools

import jax
import jax.numpy as jnp
from jax import lax
from jax.experimental import pallas as pl
from jax.experimental.pallas import tpu as pltpu
from jax.sharding import PartitionSpec as P

NZ, NH, NX, NL, NC = 8, 2, 4, 2, 2
AXES = ("dp", "tensor")
BF = jnp.bfloat16
F32 = jnp.float32
VMEM_BYTES = 16 * 1024 * 1024


def index_of(z, h, x, l, c):
    return (((z * NH + h) * NX + x) * NL + l) * NC + c


def pairs_of(move):
    pairs = []
    for z in range(NZ):
        for h in range(NH):
            for x in range(NX):
                for l in range(NL):
                    for c in range(NC):
                        pairs.append((index_of(z, h, x, l, c), index_of(*move(z, h, x, l, c))))
    return pairs


def send(value, move):
    return lax.ppermute(value, AXES, pairs_of(move))


def send_back(value, move):
    return lax.ppermute(value, AXES, [(b, a) for a, b in pairs_of(move)])


def swap_hi(z, h, x, l, c):
    return z, 1 - h, x, l, c


def swap_core(z, h, x, l, c):
    return z, h, x, l, 1 - c


def swap_plane(z, h, x, l, c):
    return z ^ 1, h, x, l, c


def along_x(step):
    return lambda z, h, x, l, c: (z, h, x ^ step, l, c)


def along_y(k):
    return lambda z, h, x, l, c: (z, h ^ (k // 2), x, l ^ (k % 2), c)


def turn(g, e=0):
    def move(z, h, x, l, c):
        return 4 * (l ^ g) + 2 * (c ^ e) + z % 2, h, x, z // 4, (z // 2) % 2

    return move


def after(value, *others):
    return lax.optimization_barrier((value, *others))[0]


def nn(a, b):
    return jnp.dot(a, b, preferred_element_type=F32)


def tn(a, b):
    return lax.dot_general(a, b, (((0,), (0,)), ((), ())), preferred_element_type=F32)


def nt(a, b):
    return lax.dot_general(a, b, (((1,), (1,)), ((), ())), preferred_element_type=F32)


def call(body, shapes, args, flops=0, where=None):
    moved = sum(a.size * a.dtype.itemsize for a in args)
    moved += sum(functools.reduce(lambda p, q: p * q, s, 1) * jnp.dtype(d).itemsize for s, d in shapes)
    scalars = [] if where is None else [where]
    return pl.pallas_call(
        body,
        out_shape=[jax.ShapeDtypeStruct(s, d) for s, d in shapes],
        in_specs=[pl.BlockSpec(memory_space=pltpu.SMEM)] * len(scalars) + [pl.BlockSpec(memory_space=pltpu.VMEM)] * len(args),
        out_specs=[pl.BlockSpec(memory_space=pltpu.VMEM)] * len(shapes),
        compiler_params=pltpu.CompilerParams(vmem_limit_bytes=VMEM_BYTES),
        cost_estimate=pl.CostEstimate(flops=flops, bytes_accessed=moved, transcendentals=0),
    )(*scalars, *args)


def blocks_of(where, fb, sub):
    t, x, b = where[0], where[2], where[3]
    for oc in range(2):
        for ol in range(2):
            rows = pl.multiple_of((t ^ (2 * ol + oc)) * sub, sub)
            for r in range(2):
                for j in range(NX):
                    s = x ^ j

                    def lanes(half, r=r, s=s):
                        return pl.multiple_of((((r ^ b) * NH + half) * NX + s) * fb, fb)

                    yield (oc * 2 + ol) * sub, (r * NX + j) * fb, rows, lanes


def pick_body(where, tok, cot, own, oth):
    sub = tok.shape[0] // 4
    fb = tok.shape[1] // 16
    h = where[1]
    for m, source in enumerate((tok, cot)):
        for to_row, to_lane, row, lanes in blocks_of(where, fb, sub):
            oth[m, to_row : to_row + sub, to_lane : to_lane + fb] = source[pl.ds(row, sub), pl.ds(lanes(1 - h), fb)]
            own[m, to_row : to_row + sub, to_lane : to_lane + fb] = source[pl.ds(row, sub), pl.ds(lanes(h), fb)]


def place_body(where, own, far, layer_out, token_grad):
    sub = own.shape[1] // 4
    fb = own.shape[2] // 8
    h = where[1]
    for m, out in enumerate((layer_out, token_grad)):
        for at_row, at_lane, row, lanes in blocks_of(where, fb, sub):
            out[pl.ds(row, sub), pl.ds(lanes(h), fb)] = own[m, at_row : at_row + sub, at_lane : at_lane + fb]
            out[pl.ds(row, sub), pl.ds(lanes(1 - h), fb)] = far[m, at_row : at_row + sub, at_lane : at_lane + fb]


def join_body(own, far, tok, cot):
    tb = own.shape[1]
    half = tb // 2
    for m, full in enumerate((tok, cot)):
        for oc in range(2):
            full[oc * tb : oc * tb + half, :] = own[m, oc * half : (oc + 1) * half, :]
            full[oc * tb + half : (oc + 1) * tb, :] = far[m, oc * half : (oc + 1) * half, :]


def forward_body(tok, cot, *refs):
    columns, (gu, dn, away) = refs[:8], refs[8:]
    tb = away.shape[0]
    fb = columns[0].shape[-1]
    for f in range(2):
        for j in range(NX):
            column = columns[f * NX + j]
            at = (f * NX + j) * fb
            for g in range(2):
                for e in range(2):
                    unit = (g * 2 + e) * fb
                    gu[at : at + fb, unit : unit + fb] = column[g, e, 0]
                    gu[at : at + fb, 4 * fb + unit : 4 * fb + unit + fb] = column[g, e, 1]
                    dn[unit : unit + fb, at : at + fb] = column[g, e, 2]
    wide = gu.shape[1]
    away[:, :wide] = nn(tok[tb:, :], gu[...]).astype(BF)
    away[:, wide:] = nt(cot[tb:, :], dn[...]).astype(BF)


def keep_body(tok, cot, gu, dn, keep):
    tb, wide = keep.shape[0], gu.shape[1]
    keep[:, :wide] = nn(tok[:tb, :], gu[...])
    keep[:, wide:] = nt(cot[:tb, :], dn[...])


def grad_body(f, da, dc, tok, cot, p1, p3, p2, p0):
    tb = da.shape[0]
    fb = p0.shape[-1]
    hid = 4 * fb
    for j, piece in ((1, p1), (3, p3), (2, p2), (0, p0)):
        at = (f * NX + j) * fb
        gu = tn(tok[:tb, at : at + fb], da[:, : 2 * hid]) + tn(tok[tb:, at : at + fb], dc[:, : 2 * hid])
        dn = tn(da[:, 2 * hid :], cot[:tb, at : at + fb]) + tn(dc[:, 2 * hid :], cot[tb:, at : at + fb])
        for g in range(2):
            for e in range(2):
                unit = (g * 2 + e) * fb
                piece[g, e, 0] = gu[:, unit : unit + fb].astype(piece.dtype)
                piece[g, e, 1] = gu[:, hid + unit : hid + unit + fb].astype(piece.dtype)
                piece[g, e, 2] = dn[unit : unit + fb].astype(piece.dtype)


def output_body(da, dc, gu, dn, own, oth):
    tb, wide = da.shape[0], gu.shape[1]
    half = tb // 2
    for oc, part in ((0, da), (1, dc)):
        out = nn(part[:, wide:], dn[...]).astype(BF)
        grad = nt(part[:, :wide], gu[...]).astype(BF)
        for m, rows in ((0, out), (1, grad)):
            own[m, oc * half : (oc + 1) * half, :] = rows[:half]
            oth[m, oc * half : (oc + 1) * half, :] = rows[half:]


def shards(tokens, gate_weight, up_weight, down_weight, cotangent):
    dp, t = lax.axis_index("dp"), lax.axis_index("tensor")
    z, h, x = dp // (NH * NX), (dp // NX) % NH, dp % NX
    where = jnp.stack([t, h, x, z % 2]).astype(jnp.int32)
    fb = gate_weight.shape[0]
    tb = tokens.shape[0]
    sub = tb // 4
    quarter = cotangent.shape[1]
    wide, hid = 8 * fb, 4 * fb

    with jax.named_scope("weights"):
        block = jnp.stack([gate_weight, up_weight, down_weight])
    with jax.named_scope("weights_turn"):
        turned = [send(block, turn(g, e)) for g in range(2) for e in range(2)]
        near = jnp.stack(turned).reshape(2, 2, *block.shape)
    with jax.named_scope("weights_plane"):
        far = send(near, swap_plane)
    where, tokens, cotangent, _ = lax.optimization_barrier((where, tokens, cotangent, block))
    with jax.named_scope("pick"):
        picked = lax.dynamic_slice(tokens, (0, t * quarter), (tb, quarter))
        own, oth = call(pick_body, [((2, tb, wide), BF)] * 2, [picked, cotangent], 0, where)
    with jax.named_scope("input_swap"):
        swapped = send(after(oth, near), swap_hi)

    def along(f, column):
        with jax.named_scope(f"weights_x_{f}"):
            return [column] + [send(column, along_x(j)) for j in range(1, NX)]

    near = along(0, near)
    far = along(1, after(far, near[1], near[3]))
    with jax.named_scope("join"):
        tok, cot = call(join_body, [((2 * tb, wide), BF)] * 2, [own, swapped])

    product = 2 * 2 * tb * wide * hid
    with jax.named_scope("forward"):
        gu, dn, away = call(
            forward_body,
            [((wide, 2 * hid), BF), ((hid, wide), BF), ((tb, 3 * hid), BF)],
            [tok, cot, *near, *far],
            3 * product // 2,
        )
        (keep,) = call(keep_body, [((tb, 3 * hid), F32)], [tok, cot, gu, dn], 3 * product // 2)
    part = keep + send(away, swap_core).astype(F32)
    pre = part[:sub]
    for k in range(1, 4):
        pre = pre + send(part[k * sub : (k + 1) * sub].astype(BF), along_y(k)).astype(F32)
    gate_pre, up_pre, d_hidden = pre[:, :hid], pre[:, hid : 2 * hid], pre[:, 2 * hid :]
    sig = jax.nn.sigmoid(gate_pre)
    act = gate_pre * sig
    hidden = (act * up_pre).astype(BF)
    d_gate = (d_hidden * up_pre * sig * (1.0 + gate_pre * (1.0 - sig))).astype(BF)
    d_up = (d_hidden * act).astype(BF)
    mine = jnp.concatenate([d_gate, d_up, hidden], axis=1)
    four = jnp.concatenate([mine] + [send(mine, along_y(k)) for k in range(1, 4)], axis=0)
    terms = (four, send(four, swap_core))

    shape = (2, 2, 3, fb, fb)

    def pieces_of(f):
        return call(functools.partial(grad_body, f), [(shape, BF)] * 3 + [(shape, F32)], [*terms, tok, cot], 3 * product // 2)

    def summed(moved, kept):
        total = kept
        for piece in moved:
            total = total + piece.astype(F32)
        return total.astype(BF)

    with jax.named_scope("grads"):
        q1, q3, q2, q0 = pieces_of(1)
        p1, p3, p2, p0 = pieces_of(0)
    with jax.named_scope("grads_x_1"):
        q1, q3, q2 = send(q1, along_x(1)), send(q3, along_x(3)), send(q2, along_x(2))
    with jax.named_scope("outputs"):
        own, oth = call(output_body, [((2, tb, wide), BF)] * 2, [*terms, gu, dn], 3 * product)
    with jax.named_scope("output_swap"):
        swapped = send(oth, swap_hi)
    with jax.named_scope("place"):
        layer_out, token_grad = call(place_body, [((tb, quarter), BF)] * 2, [own, swapped], 0, where)
    with jax.named_scope("grads_x_0"):
        p1, p3, p2 = send(p1, along_x(1)), send(p3, along_x(3)), send(p2, along_x(2))
    with jax.named_scope("grads_plane"):
        q0 = send(summed((q1, q3, q2), q0), swap_plane)
    total = after(summed((p1, p3, p2, q0), p0), swapped)
    with jax.named_scope("grads_turn"):
        pieces = [send_back(total[g, e], turn(g, e)) for g in range(2) for e in range(2)]
    *pieces, layer_out, token_grad = lax.optimization_barrier((*pieces, layer_out, token_grad))
    total = sum(piece.astype(F32) for piece in pieces)
    return layer_out, token_grad, total[0], total[1], total[2]


def solution(mesh):
    placed = (
        P("dp", None),
        P("dp", "tensor"),
        P("dp", "tensor"),
        P("tensor", "dp"),
        P("dp", "tensor"),
    )
    return jax.shard_map(
        shards,
        mesh=mesh,
        in_specs=placed,
        out_specs=(
            P("dp", "tensor"),
            P("dp", "tensor"),
            P("dp", "tensor"),
            P("dp", "tensor"),
            P("tensor", "dp"),
        ),
        check_vma=False,
    )
```
